32 devices in a mesh: groups: 2 (over x), row: 16 (over z, y, core).
Axes of the slice: x: 2, y: 2, z: 4, core: 2. Of those that a mesh axis runs over, the one named last changes fastest.
Arguments:
- atom_feat: bfloat16 [4096, 2, 128], P(('groups', 'row')), parts along dimension 0, may hold values from -6 to 6
- window_shift: int32 [128], P(('groups', 'row')), parts along dimension 0, may hold values from -16 to 16, as said below
- atom_token: int32 [4096], P('groups'), parts along dimension 0, may hold values from 0 to 255, as said below
- token_in: bfloat16 [512, 2, 768], P(('groups', 'row')), parts along dimension 0, may hold values from -6 to 6
- pair: bfloat16 [512, 256, 128], P(('groups', 'row')), parts along dimension 0, may hold values from -6 to 6
- key_mask: int32 [512], P('groups'), parts along dimension 0, may hold values from 0 to 1, as said below
- w_atom_query: bfloat16 [128, 128], replicated, may hold values from -2 to 2
- w_atom_key: bfloat16 [128, 128], replicated, may hold values from -2 to 2
- w_atom_value: bfloat16 [128, 128], replicated, may hold values from -0.5 to 0.5
- w_atom_out: bfloat16 [128, 128], replicated, may hold values from -0.5 to 0.5
- w_to_token: bfloat16 [128, 768], replicated, may hold values from -0.5 to 0.5
- w_query: bfloat16 [768, 768], replicated, may hold values from -0.21875 to 0.21875
- w_key: bfloat16 [768, 768], replicated, may hold values from -0.21875 to 0.21875
- w_value: bfloat16 [768, 768], replicated, may hold values from -0.21875 to 0.21875
- w_out: bfloat16 [768, 768], replicated, may hold values from -0.21875 to 0.21875
- w_bias: bfloat16 [128, 16], replicated, may hold values from -4 to 4
Outputs:
- atom_out: bfloat16 [4096, 2, 128], P(('groups', 'row')), parts along dimension 0
- token_out: bfloat16 [512, 2, 768], P(('groups', 'row')), parts along dimension 0
The draws below stay inside these ranges and needn't reach their ends.
There are 2 independent parts, one for each index of `groups`. The reference program is written for one: setup_inputs(seed, part) draws one part's arguments, and reference() takes and returns one part's arrays. A program takes and returns all parts, laid end to end along the dimension named above; an argument that names none is the same for every part. Nothing has to cross between parts.
Inputs may be any that keep to these rules, and one draw needn't show every extreme that they name: `window_shift`: one entry per query block, moving its key window. `atom_token`: never falls along the atoms; token 0 starts at atom 0 and token t's first atom is 8 t + r with r from -3 to 3, and with r from 1 to 3 where t is a positive multiple of 16. `key_mask`: token 0 is always kept.
All inputs are finite; a program needn't handle non-finite values.
Results may differ from the reference program's by a relative error of at most 0.0095.
Values may be sent and summed in bfloat16 or wider, within the bound.
A program may use at most 64 MiB of HBM per device.

```python
import math
import jax
import jax.numpy as jnp
from jax import lax

C_ATOM = 128
ATOM_HEADS = 4
QBLOCK = 32
KWIN = 128
SHIFT = 16
C_TOKEN = 768
TOKEN_HEADS = 16
C_PAIR = 128
SAMPLES = 2
TOK_DEV = 16
ATOMS = 2048
TOKENS = 256


atom_gap = 0.008


pair_gap = 0.0083


bias_lift = 40.0


def sign_rows(width):
    position = jnp.arange(width, dtype=jnp.int32)
    alternate = (1 - 2 * (position % 2)).astype(jnp.float32)
    paired = (1 - 2 * (position // 2 % 2)).astype(jnp.float32)
    return (alternate, paired)


def atom_lift():
    return math.sqrt(255.0 * math.sqrt(C_ATOM // ATOM_HEADS))


def atom_column(key):
    return jax.random.randint(jax.random.fold_in(key, 11), (), 0, C_ATOM)


def clipped_weight(key, fan_rows, out_cols):
    values = jnp.clip(jax.random.normal(key, (fan_rows, out_cols), jnp.float32), -5.0, 5.0)
    return values / math.sqrt(fan_rows)


def draw_w_atom_query(key, part):
    random_part = clipped_weight(jax.random.fold_in(key, 21), C_ATOM, C_ATOM)
    alternate, paired = sign_rows(C_ATOM)
    picked = jnp.arange(C_ATOM, dtype=jnp.int32)[None, :] == atom_column(key)
    special = atom_lift() / C_ATOM * alternate[:, None] + 0.05 * random_part
    return jnp.where(picked, special, random_part).astype(jnp.bfloat16)


def draw_w_atom_key(key, part):
    random_part = clipped_weight(jax.random.fold_in(key, 22), C_ATOM, C_ATOM)
    alternate, paired = sign_rows(C_ATOM)
    picked = jnp.arange(C_ATOM, dtype=jnp.int32)[None, :] == atom_column(key)
    special = atom_lift() / C_ATOM * (alternate + paired)[:, None] + 0.05 * random_part
    return jnp.where(picked, special, random_part).astype(jnp.bfloat16)


def draw_w_bias(key, part):
    random_part = clipped_weight(jax.random.fold_in(key, 31), C_PAIR, TOKEN_HEADS)
    alternate, paired = sign_rows(C_PAIR)
    chosen = jax.random.randint(jax.random.fold_in(key, 32), (), 0, TOKEN_HEADS)
    picked = jnp.arange(TOKEN_HEADS, dtype=jnp.int32)[None, :] == chosen
    lifted = random_part + bias_lift / C_PAIR * alternate[:, None]
    return jnp.where(picked, lifted, random_part).astype(jnp.bfloat16)


def draw_atom_feat(key, part):
    extent = (ATOMS, SAMPLES, C_ATOM)
    values = jax.random.normal(jax.random.fold_in(key, 41), extent, jnp.float32)
    alternate, paired = sign_rows(C_ATOM)
    strength = jnp.array([1.0, 0.85, 0.7, 1.0], jnp.float32)[:, None, None]
    places = jax.random.permutation(jax.random.fold_in(key, 43), ATOMS // 2)[:4] * 2
    noise = jax.random.normal(jax.random.fold_in(key, 44), (2, 4, SAMPLES, C_ATOM), jnp.float32)
    noise = noise - jnp.sum(noise * alternate, axis=-1, keepdims=True) / C_ATOM * alternate
    noise = noise - jnp.sum(noise * paired, axis=-1, keepdims=True) / C_ATOM * paired
    leading = strength * alternate + jnp.sqrt(1.0 - strength ** 2) * noise[0]
    shared = strength * (1.0 - atom_gap) / 2.0
    trailing = shared * (alternate + paired) + jnp.sqrt(1.0 - 2.0 * shared ** 2) * noise[1]
    values = values.at[places].set(1.5 * leading).at[places + 1].set(1.5 * trailing)
    return jnp.clip(values, -6.0, 6.0).astype(jnp.bfloat16)


def draw_pair(key, part):
    extent = (TOKENS, TOKENS, C_PAIR)
    values = jax.random.normal(jax.random.fold_in(key, 51), extent, jnp.float32)
    alternate, paired = sign_rows(C_PAIR)
    strength = jnp.array([6.0, 6.0, 5.0, 4.0], jnp.float32)
    rows_hit = jax.random.permutation(jax.random.fold_in(key, 53), TOKENS)[:4]
    near_cols = jax.random.randint(jax.random.fold_in(key, 54), (4,), 1, TOKENS).at[0].set(0)
    far_cols = (near_cols + jax.random.randint(jax.random.fold_in(key, 55), (4,), 1, TOKENS)) % TOKENS
    values = values.at[rows_hit, near_cols].set(strength[:, None] * alternate[None, :])
    values = values.at[rows_hit, far_cols].set((strength * (1.0 - pair_gap))[:, None] * alternate[None, :])
    return jnp.clip(values, -6.0, 6.0).astype(jnp.bfloat16)


def draw_window_shift(key, part):
    count = ATOMS // QBLOCK
    moves = jax.random.randint(key, (count,), -SHIFT, SHIFT + 1).astype(jnp.int32)
    return moves.at[0].set(SHIFT).at[count - 1].set(-SHIFT)


def draw_atom_token(key, part):
    jitter = jax.random.randint(jax.random.fold_in(key, 61), (TOKENS,), -3, 4).astype(jnp.int32)
    edge = jax.random.randint(jax.random.fold_in(key, 62), (TOKENS,), 1, 4).astype(jnp.int32)
    position = jnp.arange(TOKENS, dtype=jnp.int32)
    jitter = jnp.where(position % TOK_DEV == 0, edge, jitter)
    jitter = jitter.at[0].set(0).at[1].set(-3).at[2].set(3).at[TOK_DEV].set(3).at[2 * TOK_DEV].set(1)
    starts = 8 * position + jitter
    marker = jnp.zeros((ATOMS,), jnp.int32).at[starts[1:]].set(1)
    return jnp.cumsum(marker).astype(jnp.int32)


def draw_key_mask(key, part):
    flags = (jax.random.randint(key, (TOKENS,), 0, 8) < 7).astype(jnp.int32)
    return flags.at[0].set(1)


def levels(key, shape, shards, least, high):
    level, own = 1.0, jax.random.fold_in(key, 6)
    for dim, shards_of in shards:
        steps = jnp.exp(jax.random.uniform(jax.random.fold_in(own, dim), (shards_of,), jnp.float32, least / len(shards), high / len(shards)))
        level = level * jnp.repeat(steps, shape[dim] // shards_of).reshape([-1 if axis == dim else 1 for axis in range(len(shape))])
    return level


def bell_draw(stream_key, shape, scale, limit, shards=(), kind=jnp.bfloat16):
    loudness = levels(stream_key, shape, shards, -0.22, 0.18) if shards else 1.0
    drawn = jax.random.normal(stream_key, shape, jnp.float32) * scale * loudness
    return jnp.minimum(jnp.maximum(drawn, -limit), limit).astype(kind)


def setup_inputs(seed: int = 0, part: int = 0) -> dict:
    keys = jax.random.split(jax.random.key(seed), 17)
    part_splits = jax.random.split(jax.random.fold_in(keys[16], part), 17)
    atom_feat = draw_atom_feat(jax.random.fold_in(jax.random.fold_in(keys[16], part), 71), part)
    window_shift = draw_window_shift(jax.random.fold_in(jax.random.fold_in(keys[16], part), 71), part)
    atom_token = draw_atom_token(jax.random.fold_in(jax.random.fold_in(keys[16], part), 71), part)
    token_in = bell_draw(part_splits[3], (TOKENS, SAMPLES, C_TOKEN), 1.0, 6.0, ((0, 16),))
    pair = draw_pair(jax.random.fold_in(jax.random.fold_in(keys[16], part), 71), part)
    key_mask = draw_key_mask(jax.random.fold_in(jax.random.fold_in(keys[16], part), 71), part)
    w_atom_query = draw_w_atom_query(jax.random.fold_in(keys[16], 71), part)
    w_atom_key = draw_w_atom_key(jax.random.fold_in(keys[16], 71), part)
    w_atom_value = bell_draw(keys[8], (C_ATOM, C_ATOM), C_ATOM ** -0.5, 0.5)
    w_atom_out = bell_draw(keys[9], (C_ATOM, C_ATOM), C_ATOM ** -0.5, 0.5)
    w_to_token = bell_draw(keys[10], (C_ATOM, C_TOKEN), C_ATOM ** -0.5, 0.5)
    w_query = bell_draw(keys[11], (C_TOKEN, C_TOKEN), C_TOKEN ** -0.5, 0.21875)
    w_key = bell_draw(keys[12], (C_TOKEN, C_TOKEN), C_TOKEN ** -0.5, 0.21875)
    w_value = bell_draw(keys[13], (C_TOKEN, C_TOKEN), C_TOKEN ** -0.5, 0.21875)
    w_out = bell_draw(keys[14], (C_TOKEN, C_TOKEN), C_TOKEN ** -0.5, 0.21875)
    w_bias = draw_w_bias(jax.random.fold_in(keys[16], 71), part)
    return {"atom_feat": atom_feat, "window_shift": window_shift, "atom_token": atom_token, "token_in": token_in, "pair": pair, "key_mask": key_mask, "w_atom_query": w_atom_query, "w_atom_key": w_atom_key, "w_atom_value": w_atom_value, "w_atom_out": w_atom_out, "w_to_token": w_to_token, "w_query": w_query, "w_key": w_key, "w_value": w_value, "w_out": w_out, "w_bias": w_bias}


def layer_norm(x):
    x = x.astype(jnp.float32)
    mean = lax.optimization_barrier(jnp.mean(x, axis=-1, keepdims=True))
    var = lax.optimization_barrier(jnp.mean((x - mean) ** 2, axis=-1, keepdims=True))
    return (x - mean) / jnp.sqrt(var + 1e-05)

def project(x, weight):
    return jnp.einsum('asc,cd->asd', x.astype(jnp.float32), weight.astype(jnp.float32), precision=lax.Precision.HIGHEST)

def reference(atom_feat, window_shift, atom_token, token_in, pair, key_mask, w_atom_query, w_atom_key, w_atom_value, w_atom_out, w_to_token, w_query, w_key, w_value, w_out, w_bias):
    high = lax.Precision.HIGHEST
    normed = layer_norm(atom_feat).astype(jnp.bfloat16)
    query = project(normed, w_atom_query).astype(jnp.bfloat16)
    keyed = project(normed, w_atom_key).astype(jnp.bfloat16)
    valued = project(normed, w_atom_value).astype(jnp.bfloat16)
    blocks = ATOMS // QBLOCK
    margin = (KWIN - QBLOCK) // 2
    border = margin + SHIFT
    starts = jnp.arange(blocks, dtype=jnp.int32) * QBLOCK - margin + window_shift
    places = starts[:, None] + jnp.arange(KWIN, dtype=jnp.int32)[None, :]
    valid = (places >= 0) & (places < ATOMS)
    padding = ((border, border), (0, 0), (0, 0))
    window_k = jnp.take(jnp.pad(keyed, padding), places + border, axis=0)
    window_v = jnp.take(jnp.pad(valued, padding), places + border, axis=0)
    head_dim = C_ATOM // ATOM_HEADS
    qblock = query.reshape(blocks, QBLOCK, SAMPLES, ATOM_HEADS, head_dim).astype(jnp.float32)
    kblock = window_k.reshape(blocks, KWIN, SAMPLES, ATOM_HEADS, head_dim).astype(jnp.float32)
    vblock = window_v.reshape(blocks, KWIN, SAMPLES, ATOM_HEADS, head_dim).astype(jnp.float32)
    scores = jnp.einsum('bqshd,bkshd->bshqk', qblock, kblock, precision=high) / jnp.sqrt(jnp.float32(head_dim))
    keep = valid[:, None, None, None, :]
    scores = jnp.where(keep, scores, -1e+30)
    top = lax.optimization_barrier(jnp.max(scores, axis=-1, keepdims=True))
    expo = jnp.where(keep, jnp.exp(scores - top), 0.0)
    total = lax.optimization_barrier(jnp.sum(expo, axis=-1))
    weights = expo.astype(jnp.bfloat16).astype(jnp.float32)
    mixed = jnp.einsum('bshqk,bkshd->bqshd', weights, vblock, precision=high)
    mixed = mixed / jnp.transpose(total, (0, 3, 1, 2))[..., None]
    mixed = mixed.astype(jnp.bfloat16).reshape(ATOMS, SAMPLES, C_ATOM)
    atom_out = (atom_feat.astype(jnp.float32) + project(mixed, w_atom_out)).astype(jnp.bfloat16)
    hidden = jax.nn.relu(project(atom_out, w_to_token))
    sums = jax.ops.segment_sum(hidden, atom_token, num_segments=TOKENS)
    counts = jax.ops.segment_sum(jnp.ones((ATOMS,), jnp.float32), atom_token, num_segments=TOKENS)
    state = (token_in.astype(jnp.float32) + sums / counts[:, None, None]).astype(jnp.bfloat16)
    tnorm = layer_norm(state).astype(jnp.bfloat16)
    tdim = C_TOKEN // TOKEN_HEADS
    tq = project(tnorm, w_query).astype(jnp.bfloat16).reshape(TOKENS, SAMPLES, TOKEN_HEADS, tdim).astype(jnp.float32)
    tk = project(tnorm, w_key).astype(jnp.bfloat16).reshape(TOKENS, SAMPLES, TOKEN_HEADS, tdim).astype(jnp.float32)
    tv = project(tnorm, w_value).astype(jnp.bfloat16).reshape(TOKENS, SAMPLES, TOKEN_HEADS, tdim).astype(jnp.float32)
    bias = jnp.einsum('qkc,ch->hqk', pair.astype(jnp.float32), w_bias.astype(jnp.float32), precision=high)
    tscore = jnp.einsum('qshd,kshd->shqk', tq, tk, precision=high) / jnp.sqrt(jnp.float32(tdim)) + bias[None]
    flags = (key_mask > 0)[None, None, None, :]
    tscore = jnp.where(flags, tscore, -1e+30)
    ttop = lax.optimization_barrier(jnp.max(tscore, axis=-1, keepdims=True))
    texp = jnp.where(flags, jnp.exp(tscore - ttop), 0.0)
    ttotal = lax.optimization_barrier(jnp.sum(texp, axis=-1))
    tmix = jnp.einsum('shqk,kshd->shqd', texp.astype(jnp.bfloat16).astype(jnp.float32), tv, precision=high)
    tmix = (tmix / ttotal[..., None]).astype(jnp.bfloat16)
    tmix = jnp.transpose(tmix, (2, 0, 1, 3)).reshape(TOKENS, SAMPLES, C_TOKEN)
    token_out = (state.astype(jnp.float32) + project(tmix, w_out)).astype(jnp.bfloat16)
    return (atom_out, token_out)
```

```python
import functools
import math

import jax
import jax.numpy as jnp
from jax import lax
from jax.experimental import pallas as pl
from jax.experimental.pallas import tpu as pltpu
from jax.sharding import PartitionSpec as P

ATOM_HEADS = 4
QBLOCK = 32
KWIN = 128
SHIFT = 16
TOKEN_HEADS = 16
LEFT = 64
RIGHT = 96
EXTRA = 16
MESH = pl.DeviceIdType.MESH
F32 = jnp.float32
BF16 = jnp.bfloat16
LOW = -1e30


def dot(a, b):
    return jnp.dot(a, b, preferred_element_type=F32)


def dot_t(a, b):
    return lax.dot_general(a, b, (((1,), (1,)), ((), ())), preferred_element_type=F32)


def normalize(values):
    mean = jnp.mean(values, axis=-1, keepdims=True)
    centred = values - mean
    var = jnp.mean(centred * centred, axis=-1, keepdims=True)
    return centred * lax.rsqrt(var + 1e-05)


def flip(index, distance):
    result = index
    bit = 1
    while bit <= distance:
        if (distance // bit) % 2:
            result = result + bit - 2 * bit * ((index // bit) % 2)
        bit *= 2
    return result


def kernel(
    n,
    shift,
    x_in,
    ids_in,
    token_in,
    pair_in,
    mask_in,
    waq_in,
    wak_in,
    wav_in,
    wao_in,
    wtt_in,
    wq_in,
    wk_in,
    wv_in,
    wo_in,
    wb_in,
    atom_out,
    token_out,
    x,
    ids,
    tin,
    pair,
    mask,
    waq,
    wak,
    wav,
    wao,
    wtt,
    wq,
    wk,
    wv,
    wo,
    wb,
    move_own,
    move_next,
    bias,
    state,
    absorbed,
    gathered,
    load_sem,
    halo_send,
    halo_recv,
    gather_send,
    gather_recv,
):
    rank = lax.axis_index("row")
    own = x_in.shape[0]
    width = waq_in.shape[0]
    samples = x_in.shape[1] // width
    tok_dev = token_in.shape[0]
    tok_width = wq_in.shape[0]
    tokens = n * tok_dev
    outers = n // 4
    core = rank % 2
    mid = (rank // 2) % 2
    outer = rank // 4

    def device(o, m, c):
        return (o * 2 + m) * 2 + c

    mid_mate = device(outer, 1 - mid, core)
    core_mate = device(outer, mid, 1 - core)

    loads = []

    def load(source, target):
        copy = pltpu.make_async_copy(source, target, load_sem.at[len(loads)])
        copy.start()
        loads.append(copy)
        return copy

    load_x = load(x_in, x.at[pl.ds(LEFT, own)])
    load_atom = [load(*p) for p in ((waq_in, waq), (wak_in, wak), (wav_in, wav))]
    load_pair = [load(wb_in, wb), load(mask_in, mask), load(pair_in, pair)]
    load_token = [load(*p) for p in ((wao_in, wao), (wtt_in, wtt), (ids_in, ids), (token_in, tin))]
    load_wq = load(wq_in, wq)
    load_wk = load(wk_in, wk)
    load_wv = load(wv_in, wv)
    load_wo = load(wo_in, wo)

    barrier = pltpu.get_barrier_semaphore()
    partners = [(rank + 1) % n, (rank + n - 1) % n, mid_mate, core_mate]
    partners += [device(flip(outer, d), mid, core) for d in range(1, outers)]
    for partner in partners:
        pl.semaphore_signal(barrier, inc=1, device_id={"row": partner}, device_id_type=MESH)
    for b in range(own // QBLOCK):
        move_own[pl.ds(8 * b, 8), :] = jnp.full((8, 128), shift[b], jnp.int32)
    pl.semaphore_wait(barrier, len(partners))

    def remote(source, target, send, recv, to):
        return pltpu.make_async_remote_copy(
            src_ref=source,
            dst_ref=target,
            send_sem=send,
            recv_sem=recv,
            device_id={"row": to},
            device_id_type=MESH,
        )

    up = (rank + 1) % n
    down = (rank + n - 1) % n
    to_right = remote(
        x_in.at[pl.ds(own - LEFT, LEFT)], x.at[pl.ds(0, LEFT)], halo_send.at[0], halo_recv.at[0], up
    )
    to_left = remote(
        x_in.at[pl.ds(0, RIGHT)],
        x.at[pl.ds(LEFT + own, RIGHT)],
        halo_send.at[1],
        halo_recv.at[1],
        down,
    )
    move_left = remote(
        move_own.at[pl.ds(0, 8)], move_next, halo_send.at[2], halo_recv.at[2], down
    )

    @pl.when(rank < n - 1)
    def _():
        to_right.start()

    @pl.when(rank > 0)
    def _():
        to_left.start()
        move_left.start()

    @pl.when(rank == 0)
    def _():
        x[pl.ds(0, LEFT), :] = jnp.zeros((LEFT, samples * width), BF16)

    @pl.when(rank == n - 1)
    def _():
        x[pl.ds(LEFT + own, RIGHT), :] = jnp.zeros((RIGHT, samples * width), BF16)
        move_next[...] = jnp.zeros((8, 128), jnp.int32)

    for copy in load_pair:
        copy.wait()
    wide = jnp.concatenate(
        [wb[...].astype(F32), jnp.zeros((wb.shape[0], 128 - TOKEN_HEADS), F32)], axis=1
    )
    wb_t = jnp.transpose(wide)[:TOKEN_HEADS].astype(BF16)
    lowered = jnp.where(mask[...] > 0, 0.0, LOW)
    for i in range(tok_dev):
        bias[:, i, :] = dot_t(wb_t, pair[i]) + lowered

    rows = own + EXTRA
    keys = LEFT + own + RIGHT
    load_x.wait()
    for copy in load_atom:
        copy.wait()

    @pl.when(rank > 0)
    def _():
        to_right.wait_recv()

    @pl.when(rank < n - 1)
    def _():
        to_left.wait_recv()
        move_left.wait_recv()

    moved = [jnp.full((QBLOCK, keys), shift[b], jnp.int32) for b in range(own // QBLOCK)]
    moved.append(jnp.broadcast_to(move_next[0:1, 0:1], (EXTRA, keys)))
    moved = jnp.concatenate(moved, axis=0)
    place = lax.broadcasted_iota(jnp.int32, (rows, keys), 1)
    query = lax.broadcasted_iota(jnp.int32, (rows, keys), 0)
    margin = (KWIN - QBLOCK) // 2
    offset = place - ((query // QBLOCK) * QBLOCK + (LEFT - margin) + moved)
    absolute = place + (rank * own - LEFT)
    keep = (offset >= 0) & (offset < KWIN) & (absolute >= 0) & (absolute < n * own)
    window = jnp.where(keep, 0.0, LOW)
    head_dim = width // ATOM_HEADS
    lane_head = lax.broadcasted_iota(jnp.int32, (rows, width), 1) // head_dim
    scale = 1.0 / math.sqrt(head_dim)
    mixes = []
    for s in range(samples):
        cols = pl.ds(s * width, width)
        normed = normalize(x[:, cols].astype(F32)).astype(BF16)
        q = dot(normed[LEFT : LEFT + rows], waq[...])
        k = dot(normed, wak[...]).astype(BF16)
        v = dot(normed, wav[...]).astype(BF16)
        stacked = jnp.concatenate(
            [jnp.where(lane_head == h, q, 0.0) for h in range(ATOM_HEADS)], axis=0
        ).astype(BF16)
        score = dot_t(stacked, k).reshape(ATOM_HEADS, rows, keys) * scale + window[None]
        expo = jnp.exp(score - jnp.max(score, axis=-1, keepdims=True))
        total = jnp.sum(expo, axis=-1, keepdims=True)
        mix = dot(expo.reshape(ATOM_HEADS * rows, keys).astype(BF16), v)
        mix = mix.reshape(ATOM_HEADS, rows, width) * (1.0 / total)
        merged = jnp.zeros((rows, width), F32)
        for h in range(ATOM_HEADS):
            merged = jnp.where(lane_head == h, mix[h], merged)
        mixes.append(merged.astype(BF16))

    for copy in load_token:
        copy.wait()
    base = rank * tok_dev
    following = jnp.where(rank < n - 1, 0, -tokens)
    own_ids = ids[pl.ds(rank, 1), :]
    next_ids = ids[pl.ds(jnp.minimum(rank + 1, n - 1), 1), :][:, :EXTRA] + following
    row_ids = jnp.concatenate([own_ids, next_ids], axis=1) - base
    member = lax.broadcasted_iota(jnp.int32, (tok_dev, rows), 0) == row_ids
    member = jnp.where(member, 1.0, 0.0)
    share = 1.0 / jnp.sum(member, axis=1, keepdims=True)
    member = member.astype(BF16)
    here = pl.ds(pl.multiple_of(rank * tok_dev, tok_dev), tok_dev)
    for s in range(samples):
        cols = pl.ds(s * width, width)
        updated = x[pl.ds(LEFT, rows), cols].astype(F32) + dot(mixes[s], wao[...])
        updated = updated.astype(BF16)
        atom_out[:, cols] = updated[:own]
        hidden = jnp.maximum(dot(updated, wtt[...]), 0.0)
        high = hidden.astype(BF16)
        low = (hidden - high.astype(F32)).astype(BF16)
        sums = dot(member, high) + dot(member, low)
        fresh = tin[:, pl.ds(s * tok_width, tok_width)].astype(F32) + sums * share
        fresh = fresh.astype(BF16)
        state[s] = fresh
        gathered[s, here, :] = normalize(fresh.astype(F32)).astype(BF16)

    sends = []

    def send_block(origin, to):
        block = gathered.at[:, pl.ds(pl.multiple_of(origin * tok_dev, tok_dev), tok_dev), :]
        copy = remote(block, block, gather_send.at[len(sends)], gather_recv.at[origin], to)
        copy.start()
        sends.append(copy)

    def await_block(origin):
        block = gathered.at[:, pl.ds(pl.multiple_of(origin * tok_dev, tok_dev), tok_dev), :]
        remote(block, block, gather_send.at[0], gather_recv.at[origin], core_mate).wait_recv()

    for d in range(1, outers):
        send_block(rank, device(flip(outer, d), mid, core))
    send_block(rank, mid_mate)
    send_block(rank, core_mate)

    tdim = tok_width // TOKEN_HEADS
    lane_token = lax.broadcasted_iota(jnp.int32, (tok_dev, tok_width), 1) // tdim
    load_wq.wait()
    load_wk.wait()
    for s in range(samples):
        q = dot(gathered[s, here, :], wq[...])
        stacked = jnp.concatenate(
            [jnp.where(lane_token == h, q, 0.0) for h in range(TOKEN_HEADS)], axis=0
        ).astype(BF16)
        absorbed[s] = dot_t(stacked, wk[...]).astype(BF16)

    for d in range(1, outers):
        origin = device(flip(outer, d), mid, core)
        await_block(origin)
        send_block(origin, mid_mate)
        send_block(origin, core_mate)
    for d in range(outers):
        origin = device(flip(outer, d), 1 - mid, core)
        await_block(origin)
        send_block(origin, core_mate)
    for d in range(outers):
        for m in (mid, 1 - mid):
            await_block(device(flip(outer, d), m, 1 - core))

    load_wv.wait()
    load_wo.wait()
    tscale = 1.0 / math.sqrt(tdim)
    for s in range(samples):
        score = dot_t(absorbed[s], gathered[s]) * tscale
        score = score + bias[...].reshape(TOKEN_HEADS * tok_dev, tokens)
        expo = jnp.exp(score - jnp.max(score, axis=-1, keepdims=True))
        total = jnp.sum(expo, axis=-1, keepdims=True)
        v = dot(gathered[s], wv[...]).astype(BF16)
        mix = dot(expo.astype(BF16), v) * (1.0 / total)
        merged = jnp.zeros((tok_dev, tok_width), F32)
        for h in range(TOKEN_HEADS):
            merged = jnp.where(lane_token == h, mix[h * tok_dev : (h + 1) * tok_dev], merged)
        result = state[s].astype(F32) + dot(merged.astype(BF16), wo[...])
        token_out[:, pl.ds(s * tok_width, tok_width)] = result.astype(BF16)

    for copy in sends:
        copy.wait_send()

    @pl.when(rank < n - 1)
    def _():
        to_right.wait_send()

    @pl.when(rank > 0)
    def _():
        to_left.wait_send()
        move_left.wait_send()


def on_device(
    n,
    atom_feat,
    window_shift,
    atom_token,
    token_in,
    pair,
    key_mask,
    w_atom_query,
    w_atom_key,
    w_atom_value,
    w_atom_out,
    w_to_token,
    w_query,
    w_key,
    w_value,
    w_out,
    w_bias,
):
    own, samples, width = atom_feat.shape
    tok_dev, _, tok_width = token_in.shape
    tokens = pair.shape[1]
    x = atom_feat.reshape(own, samples * width)
    tin = token_in.reshape(tok_dev, samples * tok_width)
    ids = atom_token.reshape(n, own)
    mask = key_mask.reshape(1, tokens)
    big = (x, ids, tin, pair, mask, w_atom_query, w_atom_key, w_atom_value, w_atom_out)
    big += (w_to_token, w_query, w_key, w_value, w_out, w_bias)
    buffers = [pltpu.VMEM(a.shape, a.dtype) for a in big]
    buffers[0] = pltpu.VMEM((LEFT + own + RIGHT, samples * width), BF16)
    atoms, toks = pl.pallas_call(
        functools.partial(kernel, n),
        out_shape=(
            jax.ShapeDtypeStruct(x.shape, BF16),
            jax.ShapeDtypeStruct(tin.shape, BF16),
        ),
        in_specs=[pl.BlockSpec(memory_space=pltpu.SMEM)]
        + [pl.BlockSpec(memory_space=pl.ANY)] * len(big),
        out_specs=(
            pl.BlockSpec(memory_space=pltpu.VMEM),
            pl.BlockSpec(memory_space=pltpu.VMEM),
        ),
        scratch_shapes=buffers
        + [
            pltpu.VMEM((8 * (own // QBLOCK), 128), jnp.int32),
            pltpu.VMEM((8, 128), jnp.int32),
            pltpu.VMEM((TOKEN_HEADS, tok_dev, tokens), F32),
            pltpu.VMEM((samples, tok_dev, tok_width), BF16),
            pltpu.VMEM((samples, TOKEN_HEADS * tok_dev, tok_width), BF16),
            pltpu.VMEM((samples, tokens, tok_width), BF16),
            pltpu.SemaphoreType.DMA((len(big),)),
            pltpu.SemaphoreType.DMA((3,)),
            pltpu.SemaphoreType.DMA((3,)),
            pltpu.SemaphoreType.DMA((n - 1,)),
            pltpu.SemaphoreType.DMA((n,)),
        ],
        compiler_params=pltpu.CompilerParams(
            collective_id=0, has_side_effects=True, vmem_limit_bytes=48 * 1024 * 1024
        ),
    )(window_shift, *big)
    return atoms.reshape(atom_feat.shape), toks.reshape(token_in.shape)


def solution(mesh):
    rows = P(("groups", "row"), None, None)
    return jax.shard_map(
        functools.partial(on_device, mesh.shape["row"]),
        mesh=mesh,
        in_specs=(rows, P(("groups", "row")), P("groups"), rows, rows, P("groups"))
        + (P(),) * 10,
        out_specs=(rows, rows),
        check_vma=False,
    )
```

```python
import functools
import math

import jax
import jax.numpy as jnp
from jax import lax
from jax.experimental import pallas as pl
from jax.experimental.pallas import tpu as pltpu
from jax.sharding import PartitionSpec as P

ATOM_HEADS = 4
QBLOCK = 32
KWIN = 128
SHIFT = 16
TOKEN_HEADS = 16
LEFT = 64
RIGHT = 96
EXTRA = 16
MESH = pl.DeviceIdType.MESH
F32 = jnp.float32
BF16 = jnp.bfloat16
LOW = -1e30


def dot(a, b):
    return jnp.dot(a, b, preferred_element_type=F32)


def dot_t(a, b):
    return lax.dot_general(a, b, (((1,), (1,)), ((), ())), preferred_element_type=F32)


def normalize(values):
    mean = jnp.mean(values, axis=-1, keepdims=True)
    centred = values - mean
    var = jnp.mean(centred * centred, axis=-1, keepdims=True)
    return centred * lax.rsqrt(var + 1e-05)


def flip(index, distance):
    result = index
    bit = 1
    while bit <= distance:
        if (distance // bit) % 2:
            result = result + bit - 2 * bit * ((index // bit) % 2)
        bit *= 2
    return result


def kernel(
    n,
    shift,
    x_in,
    ids_in,
    token_in,
    pair_in,
    mask_in,
    waq_in,
    wak_in,
    wav_in,
    wao_in,
    wtt_in,
    wq_in,
    wk_in,
    wv_in,
    wo_in,
    wb_in,
    atom_out,
    token_out,
    x,
    ids,
    tin,
    pair,
    mask,
    waq,
    wak,
    wav,
    wao,
    wtt,
    wq,
    wk,
    wv,
    wo,
    wb,
    move_own,
    move_next,
    bias,
    atoms,
    inner,
    state,
    absorbed,
    gathered,
    load_sem,
    halo_send,
    halo_recv,
    gather_send,
    gather_recv,
):
    rank = lax.axis_index("row")
    own = x_in.shape[0]
    width = waq_in.shape[0]
    samples = x_in.shape[1]
    tok_dev = token_in.shape[0]
    tok_width = wq_in.shape[0]
    tokens = n * tok_dev
    outers = n // 4
    core = rank % 2
    mid = (rank // 2) % 2
    outer = rank // 4

    def device(o, m, c):
        return (o * 2 + m) * 2 + c

    mid_mate = device(outer, 1 - mid, core)
    core_mate = device(outer, mid, 1 - core)

    loads = []

    def load(source, target):
        copy = pltpu.make_async_copy(source, target, load_sem.at[len(loads)])
        copy.start()
        loads.append(copy)
        return copy

    load_x = load(x_in, x.at[pl.ds(LEFT, own)])
    load_atom = [load(*p) for p in ((waq_in, waq), (wak_in, wak), (wav_in, wav))]
    load_pair = [load(wb_in, wb), load(mask_in, mask), load(pair_in, pair)]
    load_token = [load(*p) for p in ((wao_in, wao), (wtt_in, wtt), (ids_in, ids), (token_in, tin))]
    load_wq = load(wq_in, wq)
    load_wk = load(wk_in, wk)
    load_wv = load(wv_in, wv)
    load_wo = load(wo_in, wo)

    barrier = pltpu.get_barrier_semaphore()
    partners = [(rank + 1) % n, (rank + n - 1) % n, mid_mate, core_mate]
    partners += [device(flip(outer, d), mid, core) for d in range(1, outers)]
    for partner in partners:
        pl.semaphore_signal(barrier, inc=1, device_id={"row": partner}, device_id_type=MESH)
    for b in range(own // QBLOCK):
        move_own[pl.ds(8 * b, 8), :] = jnp.full((8, 128), shift[b], jnp.int32)
    pl.semaphore_wait(barrier, len(partners))

    def remote(source, target, send, recv, to):
        return pltpu.make_async_remote_copy(
            src_ref=source,
            dst_ref=target,
            send_sem=send,
            recv_sem=recv,
            device_id={"row": to},
            device_id_type=MESH,
        )

    up = (rank + 1) % n
    down = (rank + n - 1) % n
    to_right = remote(
        x_in.at[pl.ds(own - LEFT, LEFT)], x.at[pl.ds(0, LEFT)], halo_send.at[0], halo_recv.at[0], up
    )
    to_left = remote(
        x_in.at[pl.ds(0, RIGHT)],
        x.at[pl.ds(LEFT + own, RIGHT)],
        halo_send.at[1],
        halo_recv.at[1],
        down,
    )
    move_left = remote(
        move_own.at[pl.ds(0, 8)], move_next, halo_send.at[2], halo_recv.at[2], down
    )

    @pl.when(rank < n - 1)
    def _():
        to_right.start()

    @pl.when(rank > 0)
    def _():
        to_left.start()
        move_left.start()

    @pl.when(rank == 0)
    def _():
        x[pl.ds(0, LEFT)] = jnp.zeros((LEFT, samples, width), BF16)

    @pl.when(rank == n - 1)
    def _():
        x[pl.ds(LEFT + own, RIGHT)] = jnp.zeros((RIGHT, samples, width), BF16)
        move_next[...] = jnp.zeros((8, 128), jnp.int32)

    for copy in load_pair:
        copy.wait()
    wb_t = wb[...]
    lowered = jnp.where(mask[...] > 0, 0.0, LOW)
    for i in range(tok_dev):
        bias[:, i, :] = dot_t(wb_t, pair[i]) + lowered

    rows = own + EXTRA
    keys = LEFT + own + RIGHT
    load_x.wait()
    for copy in load_atom:
        copy.wait()

    @pl.when(rank > 0)
    def _():
        to_right.wait_recv()

    @pl.when(rank < n - 1)
    def _():
        to_left.wait_recv()
        move_left.wait_recv()

    moved = [jnp.full((QBLOCK, keys), shift[b], jnp.int32) for b in range(own // QBLOCK)]
    moved.append(jnp.broadcast_to(move_next[0:1, 0:1], (EXTRA, keys)))
    moved = jnp.concatenate(moved, axis=0)
    place = lax.broadcasted_iota(jnp.int32, (rows, keys), 1)
    query = lax.broadcasted_iota(jnp.int32, (rows, keys), 0)
    margin = (KWIN - QBLOCK) // 2
    offset = place - ((query // QBLOCK) * QBLOCK + (LEFT - margin) + moved)
    absolute = place + (rank * own - LEFT)
    keep = (offset >= 0) & (offset < KWIN) & (absolute >= 0) & (absolute < n * own)
    window = jnp.where(keep, 0.0, LOW)
    head_dim = width // ATOM_HEADS
    lane_head = lax.broadcasted_iota(jnp.int32, (rows, width), 1) // head_dim
    scale = 1.0 / math.sqrt(head_dim)
    atoms[...] = x[...].astype(F32).reshape(samples * keys, width)
    mixes = []
    for s in range(samples):
        normed = normalize(atoms[pl.ds(s, keys, stride=samples), :]).astype(BF16)
        q = dot(normed[LEFT : LEFT + rows], waq[...])
        k = dot(normed, wak[...]).astype(BF16)
        v = dot(normed, wav[...]).astype(BF16)
        stacked = jnp.concatenate(
            [jnp.where(lane_head == h, q, 0.0) for h in range(ATOM_HEADS)], axis=0
        ).astype(BF16)
        score = dot_t(stacked, k).reshape(ATOM_HEADS, rows, keys) * scale + window[None]
        expo = jnp.exp(score - jnp.max(score, axis=-1, keepdims=True))
        total = jnp.sum(expo, axis=-1, keepdims=True)
        mix = dot(expo.reshape(ATOM_HEADS * rows, keys).astype(BF16), v)
        mix = mix.reshape(ATOM_HEADS, rows, width) * (1.0 / total)
        merged = jnp.zeros((rows, width), F32)
        for h in range(ATOM_HEADS):
            merged = jnp.where(lane_head == h, mix[h], merged)
        mixes.append(merged.astype(BF16))

    for copy in load_token:
        copy.wait()
    base = rank * tok_dev
    following = jnp.where(rank < n - 1, 0, -tokens)
    own_ids = ids[pl.ds(rank, 1), :]
    next_ids = ids[pl.ds(jnp.minimum(rank + 1, n - 1), 1), :][:, :EXTRA] + following
    row_ids = jnp.concatenate([own_ids, next_ids], axis=1) - base
    member = lax.broadcasted_iota(jnp.int32, (tok_dev, rows), 0) == row_ids
    member = jnp.where(member, 1.0, 0.0)
    share = 1.0 / jnp.sum(member, axis=1, keepdims=True)
    member = member.astype(BF16)
    given = tin[...].astype(F32).reshape(samples * tok_dev, tok_width)
    for c in range(tok_width // 128):
        inner[c] = given[:, c * 128 : (c + 1) * 128]
    here = pl.ds(pl.multiple_of(rank * tok_dev, tok_dev), tok_dev)
    for s in range(samples):
        cols = pl.ds(s * width, width)
        updated = atoms[pl.ds(LEFT * samples + s, rows, stride=samples), :] + dot(mixes[s], wao[...])
        updated = updated.astype(BF16)
        atom_out[:, cols] = updated[:own]
        hidden = jnp.maximum(dot(updated, wtt[...]), 0.0)
        high = hidden.astype(BF16)
        low = (hidden - high.astype(F32)).astype(BF16)
        sums = dot(member, high) + dot(member, low)
        given = [
            inner[c, pl.ds(s, tok_dev, stride=samples), :] for c in range(tok_width // 128)
        ]
        fresh = jnp.concatenate(given, axis=1) + sums * share
        fresh = fresh.astype(BF16)
        state[s] = fresh
        gathered[s, here, :] = normalize(fresh.astype(F32)).astype(BF16)

    sends = []

    def send_block(origin, to):
        block = gathered.at[:, pl.ds(pl.multiple_of(origin * tok_dev, tok_dev), tok_dev), :]
        copy = remote(block, block, gather_send.at[len(sends)], gather_recv.at[origin], to)
        copy.start()
        sends.append(copy)

    def await_block(origin):
        block = gathered.at[:, pl.ds(pl.multiple_of(origin * tok_dev, tok_dev), tok_dev), :]
        remote(block, block, gather_send.at[0], gather_recv.at[origin], core_mate).wait_recv()

    for d in range(1, outers):
        send_block(rank, device(flip(outer, d), mid, core))
    send_block(rank, mid_mate)
    send_block(rank, core_mate)

    tdim = tok_width // TOKEN_HEADS
    lane_token = lax.broadcasted_iota(jnp.int32, (tok_dev, tok_width), 1) // tdim
    load_wq.wait()
    load_wk.wait()
    for s in range(samples):
        q = dot(gathered[s, here, :], wq[...])
        stacked = jnp.concatenate(
            [jnp.where(lane_token == h, q, 0.0) for h in range(TOKEN_HEADS)], axis=0
        ).astype(BF16)
        absorbed[s] = dot_t(stacked, wk[...]).astype(BF16)

    for d in range(1, outers):
        origin = device(flip(outer, d), mid, core)
        await_block(origin)
        send_block(origin, mid_mate)
        send_block(origin, core_mate)
    for d in range(outers):
        origin = device(flip(outer, d), 1 - mid, core)
        await_block(origin)
        send_block(origin, core_mate)
    for d in range(outers):
        for m in (mid, 1 - mid):
            await_block(device(flip(outer, d), m, 1 - core))

    load_wv.wait()
    load_wo.wait()
    tscale = 1.0 / math.sqrt(tdim)
    for s in range(samples):
        score = dot_t(absorbed[s], gathered[s]) * tscale
        score = score + bias[...].reshape(TOKEN_HEADS * tok_dev, tokens)
        expo = jnp.exp(score - jnp.max(score, axis=-1, keepdims=True))
        total = jnp.sum(expo, axis=-1, keepdims=True)
        v = dot(gathered[s], wv[...]).astype(BF16)
        mix = dot(expo.astype(BF16), v) * (1.0 / total)
        merged = jnp.zeros((tok_dev, tok_width), F32)
        for h in range(TOKEN_HEADS):
            merged = jnp.where(lane_token == h, mix[h * tok_dev : (h + 1) * tok_dev], merged)
        result = state[s].astype(F32) + dot(merged.astype(BF16), wo[...])
        token_out[:, pl.ds(s * tok_width, tok_width)] = result.astype(BF16)

    for copy in sends:
        copy.wait_send()

    @pl.when(rank < n - 1)
    def _():
        to_right.wait_send()

    @pl.when(rank > 0)
    def _():
        to_left.wait_send()
        move_left.wait_send()


def on_device(
    n,
    atom_feat,
    window_shift,
    atom_token,
    token_in,
    pair,
    key_mask,
    w_atom_query,
    w_atom_key,
    w_atom_value,
    w_atom_out,
    w_to_token,
    w_query,
    w_key,
    w_value,
    w_out,
    w_bias,
):
    own, samples, width = atom_feat.shape
    tok_dev, _, tok_width = token_in.shape
    tokens = pair.shape[1]
    ids = atom_token.reshape(n, own)
    mask = key_mask.reshape(1, tokens)
    big = (atom_feat, ids, token_in, pair, mask, w_atom_query, w_atom_key, w_atom_value, w_atom_out)
    big += (w_to_token, w_query, w_key, w_value, w_out, w_bias.T)
    buffers = [pltpu.VMEM(a.shape, a.dtype) for a in big]
    buffers[0] = pltpu.VMEM((LEFT + own + RIGHT, samples, width), BF16)
    atoms, toks = pl.pallas_call(
        functools.partial(kernel, n),
        out_shape=(
            jax.ShapeDtypeStruct((own, samples * width), BF16),
            jax.ShapeDtypeStruct((tok_dev, samples * tok_width), BF16),
        ),
        in_specs=[pl.BlockSpec(memory_space=pltpu.SMEM)]
        + [pl.BlockSpec(memory_space=pltpu.HBM)] * len(big),
        out_specs=(
            pl.BlockSpec(memory_space=pltpu.VMEM),
            pl.BlockSpec(memory_space=pltpu.VMEM),
        ),
        scratch_shapes=buffers
        + [
            pltpu.VMEM((8 * (own // QBLOCK), 128), jnp.int32),
            pltpu.VMEM((8, 128), jnp.int32),
            pltpu.VMEM((TOKEN_HEADS, tok_dev, tokens), F32),
            pltpu.VMEM((samples * (LEFT + own + RIGHT), width), F32),
            pltpu.VMEM((tok_width // 128, samples * tok_dev, 128), F32),
            pltpu.VMEM((samples, tok_dev, tok_width), BF16),
            pltpu.VMEM((samples, TOKEN_HEADS * tok_dev, tok_width), BF16),
            pltpu.VMEM((samples, tokens, tok_width), BF16),
            pltpu.SemaphoreType.DMA((len(big),)),
            pltpu.SemaphoreType.DMA((3,)),
            pltpu.SemaphoreType.DMA((3,)),
            pltpu.SemaphoreType.DMA((n - 1,)),
            pltpu.SemaphoreType.DMA((n,)),
        ],
        compiler_params=pltpu.CompilerParams(
            collective_id=0, has_side_effects=True, vmem_limit_bytes=63 * 1024 * 1024
        ),
    )(window_shift, *big)
    return atoms.reshape(atom_feat.shape), toks.reshape(token_in.shape)


def solution(mesh):
    rows = P(("groups", "row"), None, None)
    return jax.shard_map(
        functools.partial(on_device, mesh.shape["row"]),
        mesh=mesh,
        in_specs=(rows, P(("groups", "row")), P("groups"), rows, rows, P("groups"))
        + (P(),) * 10,
        out_specs=(rows, rows),
        check_vma=False,
    )
```

```python
import functools
import math

import jax
import jax.numpy as jnp
from jax import lax
from jax.experimental import pallas as pl
from jax.experimental.pallas import tpu as pltpu
from jax.sharding import PartitionSpec as P

ATOM_HEADS = 4
QBLOCK = 32
KWIN = 128
SHIFT = 16
TOKEN_HEADS = 16
LEFT = 64
RIGHT = 96
EXTRA = 16
MESH = pl.DeviceIdType.MESH
F32 = jnp.float32
BF16 = jnp.bfloat16
LOW = -1e30


def dot(a, b):
    return jnp.dot(a, b, preferred_element_type=F32)


def dot_t(a, b):
    return lax.dot_general(a, b, (((1,), (1,)), ((), ())), preferred_element_type=F32)


def normalize(values):
    mean = jnp.mean(values, axis=-1, keepdims=True)
    centred = values - mean
    var = jnp.mean(centred * centred, axis=-1, keepdims=True)
    return centred * lax.rsqrt(var + 1e-05)


def flip(index, distance):
    result = index
    bit = 1
    while bit <= distance:
        if (distance // bit) % 2:
            result = result + bit - 2 * bit * ((index // bit) % 2)
        bit *= 2
    return result


def kernel(
    n,
    shift,
    x_in,
    ids_in,
    token_in,
    pair_in,
    mask_in,
    waq_in,
    wak_in,
    wav_in,
    wao_in,
    wtt_in,
    wq_in,
    wk_in,
    wv_in,
    wo_in,
    wb_in,
    atom_out,
    token_out,
    x,
    ids,
    tin,
    pair,
    mask,
    waq,
    wak,
    wav,
    wao,
    wtt,
    wq,
    wk,
    wv,
    wo,
    wb,
    move_own,
    move_next,
    bias,
    atoms,
    inner,
    state,
    absorbed,
    gathered,
    load_sem,
    halo_send,
    halo_recv,
    gather_send,
    gather_recv,
):
    rank = lax.axis_index("row")
    own = x_in.shape[0]
    width = waq_in.shape[0]
    samples = x_in.shape[1]
    tok_dev = token_in.shape[0]
    tok_width = wq_in.shape[0]
    tokens = n * tok_dev
    outers = n // 4
    core = rank % 2
    mid = (rank // 2) % 2
    outer = rank // 4

    def device(o, m, c):
        return (o * 2 + m) * 2 + c

    mid_mate = device(outer, 1 - mid, core)
    core_mate = device(outer, mid, 1 - core)

    loads = []

    def load(source, target):
        copy = pltpu.make_async_copy(source, target, load_sem.at[len(loads)])
        copy.start()
        loads.append(copy)
        return copy

    load_x = load(x_in, x.at[pl.ds(LEFT, own)])
    load_atom = [load(*p) for p in ((waq_in, waq), (wak_in, wak), (wav_in, wav))]
    load_pair = [load(wb_in, wb), load(mask_in, mask), load(pair_in, pair)]
    load_token = [load(*p) for p in ((wao_in, wao), (wtt_in, wtt), (ids_in, ids), (token_in, tin))]
    load_wq = load(wq_in, wq)
    load_wk = load(wk_in, wk)
    load_wv = load(wv_in, wv)
    load_wo = load(wo_in, wo)

    barrier = pltpu.get_barrier_semaphore()
    partners = [(rank + 1) % n, (rank + n - 1) % n, mid_mate, core_mate]
    partners += [device(flip(outer, d), mid, core) for d in range(1, outers)]
    for partner in partners:
        pl.semaphore_signal(barrier, inc=1, device_id={"row": partner}, device_id_type=MESH)
    for b in range(own // QBLOCK):
        move_own[pl.ds(8 * b, 8), :] = jnp.full((8, 128), shift[b], jnp.int32)
    pl.semaphore_wait(barrier, len(partners))

    def remote(source, target, send, recv, to):
        return pltpu.make_async_remote_copy(
            src_ref=source,
            dst_ref=target,
            send_sem=send,
            recv_sem=recv,
            device_id={"row": to},
            device_id_type=MESH,
        )

    up = (rank + 1) % n
    down = (rank + n - 1) % n
    to_right = remote(
        x_in.at[pl.ds(own - LEFT, LEFT)], x.at[pl.ds(0, LEFT)], halo_send.at[0], halo_recv.at[0], up
    )
    to_left = remote(
        x_in.at[pl.ds(0, RIGHT)],
        x.at[pl.ds(LEFT + own, RIGHT)],
        halo_send.at[1],
        halo_recv.at[1],
        down,
    )
    move_left = remote(
        move_own.at[pl.ds(0, 8)], move_next, halo_send.at[2], halo_recv.at[2], down
    )

    @pl.when(rank < n - 1)
    def _():
        to_right.start()

    @pl.when(rank > 0)
    def _():
        to_left.start()
        move_left.start()

    @pl.when(rank == 0)
    def _():
        x[pl.ds(0, LEFT)] = jnp.zeros((LEFT, samples, width), BF16)

    @pl.when(rank == n - 1)
    def _():
        x[pl.ds(LEFT + own, RIGHT)] = jnp.zeros((RIGHT, samples, width), BF16)
        move_next[...] = jnp.zeros((8, 128), jnp.int32)

    rows = own + EXTRA
    keys = LEFT + own + RIGHT
    load_x.wait()
    for copy in load_atom:
        copy.wait()

    @pl.when(rank > 0)
    def _():
        to_right.wait_recv()

    @pl.when(rank < n - 1)
    def _():
        to_left.wait_recv()
        move_left.wait_recv()

    moved = [jnp.full((QBLOCK, keys), shift[b], jnp.int32) for b in range(own // QBLOCK)]
    moved.append(jnp.broadcast_to(move_next[0:1, 0:1], (EXTRA, keys)))
    moved = jnp.concatenate(moved, axis=0)
    place = lax.broadcasted_iota(jnp.int32, (rows, keys), 1)
    query = lax.broadcasted_iota(jnp.int32, (rows, keys), 0)
    margin = (KWIN - QBLOCK) // 2
    offset = place - ((query // QBLOCK) * QBLOCK + (LEFT - margin) + moved)
    absolute = place + (rank * own - LEFT)
    keep = (offset >= 0) & (offset < KWIN) & (absolute >= 0) & (absolute < n * own)
    window = jnp.where(keep, 0.0, LOW)
    head_dim = width // ATOM_HEADS
    lane_head = lax.broadcasted_iota(jnp.int32, (rows, width), 1) // head_dim
    scale = 1.0 / math.sqrt(head_dim)
    atoms[...] = x[...].astype(F32).reshape(samples * keys, width)
    mixes = []
    for s in range(samples):
        normed = normalize(atoms[pl.ds(s, keys, stride=samples), :]).astype(BF16)
        q = dot(normed[LEFT : LEFT + rows], waq[...])
        k = dot(normed, wak[...]).astype(BF16)
        v = dot(normed, wav[...]).astype(BF16)
        stacked = jnp.concatenate(
            [jnp.where(lane_head == h, q, 0.0) for h in range(ATOM_HEADS)], axis=0
        ).astype(BF16)
        score = dot_t(stacked, k).reshape(ATOM_HEADS, rows, keys) * scale + window[None]
        expo = jnp.exp(score - jnp.max(score, axis=-1, keepdims=True))
        total = jnp.sum(expo, axis=-1, keepdims=True)
        mix = dot(expo.reshape(ATOM_HEADS * rows, keys).astype(BF16), v)
        mix = mix.reshape(ATOM_HEADS, rows, width) * (1.0 / total)
        merged = jnp.zeros((rows, width), F32)
        for h in range(ATOM_HEADS):
            merged = jnp.where(lane_head == h, mix[h], merged)
        mixes.append(merged.astype(BF16))

    for copy in load_token:
        copy.wait()
    base = rank * tok_dev
    following = jnp.where(rank < n - 1, 0, -tokens)
    own_ids = ids[pl.ds(rank, 1), :]
    next_ids = ids[pl.ds(jnp.minimum(rank + 1, n - 1), 1), :][:, :EXTRA] + following
    row_ids = jnp.concatenate([own_ids, next_ids], axis=1) - base
    member = lax.broadcasted_iota(jnp.int32, (tok_dev, rows), 0) == row_ids
    member = jnp.where(member, 1.0, 0.0)
    share = 1.0 / jnp.sum(member, axis=1, keepdims=True)
    member = member.astype(BF16)
    given = tin[...].astype(F32).reshape(samples * tok_dev, tok_width)
    for c in range(tok_width // 128):
        inner[c] = given[:, c * 128 : (c + 1) * 128]
    here = pl.ds(pl.multiple_of(rank * tok_dev, tok_dev), tok_dev)
    sends = []

    def block_of(s, origin):
        return gathered.at[s, pl.ds(pl.multiple_of(origin * tok_dev, tok_dev), tok_dev), :]

    def send_block(s, origin, to):
        block = block_of(s, origin)
        copy = remote(
            block, block, gather_send.at[len(sends)], gather_recv.at[s * n + origin], to
        )
        copy.start()
        sends.append(copy)

    def await_block(s, origin):
        block = block_of(s, origin)
        remote(
            block, block, gather_send.at[0], gather_recv.at[s * n + origin], core_mate
        ).wait_recv()

    for s in range(samples):
        updated = atoms[pl.ds(LEFT * samples + s, rows, stride=samples), :]
        updated = (updated + dot(mixes[s], wao[...])).astype(BF16)
        atoms[pl.ds(LEFT * samples + s, rows, stride=samples), :] = updated.astype(F32)
        hidden = jnp.maximum(dot(updated, wtt[...]), 0.0)
        high = hidden.astype(BF16)
        low = (hidden - high.astype(F32)).astype(BF16)
        sums = dot(member, high) + dot(member, low)
        given = [
            inner[c, pl.ds(s, tok_dev, stride=samples), :] for c in range(tok_width // 128)
        ]
        fresh = (jnp.concatenate(given, axis=1) + sums * share).astype(BF16)
        state[s] = fresh
        gathered[s, here, :] = normalize(fresh.astype(F32)).astype(BF16)
        for d in range(1, outers):
            send_block(s, rank, device(flip(outer, d), mid, core))
        send_block(s, rank, mid_mate)
        send_block(s, rank, core_mate)

    tdim = tok_width // TOKEN_HEADS
    lane_token = lax.broadcasted_iota(jnp.int32, (tok_dev, tok_width), 1) // tdim

    def absorb(s):
        q = dot(gathered[s, here, :], wq[...])
        stacked = jnp.concatenate(
            [jnp.where(lane_token == h, q, 0.0) for h in range(TOKEN_HEADS)], axis=0
        ).astype(BF16)
        absorbed[s] = dot_t(stacked, wk[...]).astype(BF16)

    def bias_rows(first, count):
        wb_t = wb[...]
        lowered = jnp.where(mask[...] > 0, 0.0, LOW)
        for i in range(first, first + count):
            bias[:, i, :] = dot_t(wb_t, pair[i]) + lowered

    def relay_outer(s):
        for d in range(1, outers):
            origin = device(flip(outer, d), mid, core)
            await_block(s, origin)
            send_block(s, origin, mid_mate)
            send_block(s, origin, core_mate)

    def relay_mid(s):
        for d in range(outers):
            origin = device(flip(outer, d), 1 - mid, core)
            await_block(s, origin)
            send_block(s, origin, core_mate)

    load_wq.wait()
    load_wk.wait()
    for copy in load_pair:
        copy.wait()
    quarter = tok_dev // 4
    absorb(0)
    relay_outer(0)
    bias_rows(0, quarter)
    relay_outer(1)
    bias_rows(quarter, quarter)
    relay_mid(0)
    absorb(1)
    relay_mid(1)
    bias_rows(2 * quarter, 2 * quarter)
    atom_out[...] = (
        atoms[pl.ds(LEFT * samples, own * samples), :].reshape(own, samples, width).astype(BF16)
    )

    load_wv.wait()
    load_wo.wait()
    tscale = 1.0 / math.sqrt(tdim)
    for s in range(samples):
        for d in range(outers):
            for m in (mid, 1 - mid):
                await_block(s, device(flip(outer, d), m, 1 - core))
        score = dot_t(absorbed[s], gathered[s]) * tscale
        score = score + bias[...].reshape(TOKEN_HEADS * tok_dev, tokens)
        expo = jnp.exp(score - jnp.max(score, axis=-1, keepdims=True))
        total = jnp.sum(expo, axis=-1, keepdims=True)
        v = dot(gathered[s], wv[...]).astype(BF16)
        mix = dot(expo.astype(BF16), v) * (1.0 / total)
        merged = jnp.zeros((tok_dev, tok_width), F32)
        for h in range(TOKEN_HEADS):
            merged = jnp.where(lane_token == h, mix[h * tok_dev : (h + 1) * tok_dev], merged)
        result = state[s].astype(F32) + dot(merged.astype(BF16), wo[...])
        for c in range(tok_width // 128):
            inner[c, pl.ds(s, tok_dev, stride=samples), :] = result[:, c * 128 : (c + 1) * 128]
    result = jnp.concatenate([inner[c] for c in range(tok_width // 128)], axis=1)
    token_out[...] = result.reshape(tok_dev, samples, tok_width).astype(BF16)

    for copy in sends:
        copy.wait_send()

    @pl.when(rank < n - 1)
    def _():
        to_right.wait_send()

    @pl.when(rank > 0)
    def _():
        to_left.wait_send()
        move_left.wait_send()


def on_device(
    n,
    atom_feat,
    window_shift,
    atom_token,
    token_in,
    pair,
    key_mask,
    w_atom_query,
    w_atom_key,
    w_atom_value,
    w_atom_out,
    w_to_token,
    w_query,
    w_key,
    w_value,
    w_out,
    w_bias,
):
    own, samples, width = atom_feat.shape
    tok_dev, _, tok_width = token_in.shape
    tokens = pair.shape[1]
    ids = atom_token.reshape(n, own)
    mask = key_mask.reshape(1, tokens)
    big = (atom_feat, ids, token_in, pair, mask, w_atom_query, w_atom_key, w_atom_value, w_atom_out)
    big += (w_to_token, w_query, w_key, w_value, w_out, w_bias.T)
    buffers = [pltpu.VMEM(a.shape, a.dtype) for a in big]
    buffers[0] = pltpu.VMEM((LEFT + own + RIGHT, samples, width), BF16)
    atoms, toks = pl.pallas_call(
        functools.partial(kernel, n),
        out_shape=(
            pltpu.VMEM(atom_feat.shape, BF16),
            pltpu.VMEM(token_in.shape, BF16),
        ),
        in_specs=[pl.BlockSpec(memory_space=pltpu.SMEM)]
        + [pl.BlockSpec(memory_space=pltpu.HBM)] * len(big),
        out_specs=(
            pl.BlockSpec(memory_space=pltpu.VMEM),
            pl.BlockSpec(memory_space=pltpu.VMEM),
        ),
        scratch_shapes=buffers
        + [
            pltpu.VMEM((8 * (own // QBLOCK), 128), jnp.int32),
            pltpu.VMEM((8, 128), jnp.int32),
            pltpu.VMEM((TOKEN_HEADS, tok_dev, tokens), F32),
            pltpu.VMEM((samples * (LEFT + own + RIGHT), width), F32),
            pltpu.VMEM((tok_width // 128, samples * tok_dev, 128), F32),
            pltpu.VMEM((samples, tok_dev, tok_width), BF16),
            pltpu.VMEM((samples, TOKEN_HEADS * tok_dev, tok_width), BF16),
            pltpu.VMEM((samples, tokens, tok_width), BF16),
            pltpu.SemaphoreType.DMA((len(big),)),
            pltpu.SemaphoreType.DMA((3,)),
            pltpu.SemaphoreType.DMA((3,)),
            pltpu.SemaphoreType.DMA((samples * (n - 1),)),
            pltpu.SemaphoreType.DMA((samples * n,)),
        ],
        compiler_params=pltpu.CompilerParams(
            collective_id=0, has_side_effects=True, vmem_limit_bytes=48 * 1024 * 1024
        ),
    )(*[pltpu.with_memory_space_constraint(a, pltpu.HBM) for a in (window_shift, *big)])
    return atoms, toks


def solution(mesh):
    rows = P(("groups", "row"), None, None)
    return jax.shard_map(
        functools.partial(on_device, mesh.shape["row"]),
        mesh=mesh,
        in_specs=(rows, P(("groups", "row")), P("groups"), rows, rows, P("groups"))
        + (P(),) * 10,
        out_specs=(rows, rows),
        check_vma=False,
    )
```

```python
import functools
import math

import jax
import jax.numpy as jnp
from jax import lax
from jax.experimental import pallas as pl
from jax.experimental.pallas import tpu as pltpu
from jax.sharding import PartitionSpec as P

ATOM_HEADS = 4
QBLOCK = 32
KWIN = 128
SHIFT = 16
TOKEN_HEADS = 16
LEFT = 64
RIGHT = 96
EXTRA = 16
MESH = pl.DeviceIdType.MESH
F32 = jnp.float32
BF16 = jnp.bfloat16
LOW = -1e30


def dot(a, b):
    return jnp.dot(a, b, preferred_element_type=F32)


def dot_t(a, b):
    return lax.dot_general(a, b, (((1,), (1,)), ((), ())), preferred_element_type=F32)


def normalize(values):
    mean = jnp.mean(values, axis=-1, keepdims=True)
    centred = values - mean
    var = jnp.mean(centred * centred, axis=-1, keepdims=True)
    return centred * lax.rsqrt(var + 1e-05)


def flip(index, distance):
    result = index
    bit = 1
    while bit <= distance:
        if (distance // bit) % 2:
            result = result + bit - 2 * bit * ((index // bit) % 2)
        bit *= 2
    return result


def kernel(
    n,
    shift,
    x_in,
    ids_in,
    token_in,
    pair_in,
    mask_in,
    waq_in,
    wak_in,
    wav_in,
    wao_in,
    wtt_in,
    wq_in,
    wk_in,
    wv_in,
    wo_in,
    wb_in,
    atom_out,
    token_out,
    x,
    ids,
    tin,
    pair,
    mask,
    waq,
    wak,
    wav,
    wao,
    wtt,
    wq,
    wk,
    wv,
    wo,
    wb,
    move_own,
    move_next,
    bias,
    atoms,
    inner,
    state,
    absorbed,
    gathered,
    load_sem,
    halo_send,
    halo_recv,
    gather_send,
    gather_recv,
):
    rank = lax.axis_index("row")
    own = x_in.shape[0]
    width = waq_in.shape[0]
    samples = x_in.shape[1]
    tok_dev = token_in.shape[0]
    tok_width = wq_in.shape[0]
    tokens = n * tok_dev
    outers = n // 4
    core = rank % 2
    mid = (rank // 2) % 2
    outer = rank // 4

    def device(o, m, c):
        return (o * 2 + m) * 2 + c

    mid_mate = device(outer, 1 - mid, core)
    core_mate = device(outer, mid, 1 - core)

    loads = []

    def load(source, target):
        copy = pltpu.make_async_copy(source, target, load_sem.at[len(loads)])
        copy.start()
        loads.append(copy)
        return copy

    load_x = load(x_in, x.at[pl.ds(LEFT, own)])
    load_atom = [load(*p) for p in ((waq_in, waq), (wak_in, wak), (wav_in, wav))]
    load_pair = [load(wb_in, wb), load(mask_in, mask), load(pair_in, pair)]
    load_token = [load(*p) for p in ((wao_in, wao), (wtt_in, wtt), (ids_in, ids), (token_in, tin))]
    load_wq = load(wq_in, wq)
    load_wk = load(wk_in, wk)
    load_wv = load(wv_in, wv)
    load_wo = load(wo_in, wo)

    barrier = pltpu.get_barrier_semaphore()
    partners = [(rank + 1) % n, (rank + n - 1) % n, mid_mate, core_mate]
    partners += [device(flip(outer, d), mid, core) for d in range(1, outers)]
    for partner in partners:
        pl.semaphore_signal(barrier, inc=1, device_id={"row": partner}, device_id_type=MESH)
    for b in range(own // QBLOCK):
        move_own[pl.ds(8 * b, 8), :] = jnp.full((8, 128), shift[b], jnp.int32)
    pl.semaphore_wait(barrier, len(partners))

    def remote(source, target, send, recv, to):
        return pltpu.make_async_remote_copy(
            src_ref=source,
            dst_ref=target,
            send_sem=send,
            recv_sem=recv,
            device_id={"row": to},
            device_id_type=MESH,
        )

    up = (rank + 1) % n
    down = (rank + n - 1) % n
    to_right = remote(
        x_in.at[pl.ds(own - LEFT, LEFT)], x.at[pl.ds(0, LEFT)], halo_send.at[0], halo_recv.at[0], up
    )
    to_left = remote(
        x_in.at[pl.ds(0, RIGHT)],
        x.at[pl.ds(LEFT + own, RIGHT)],
        halo_send.at[1],
        halo_recv.at[1],
        down,
    )
    move_left = remote(
        move_own.at[pl.ds(0, 8)], move_next, halo_send.at[2], halo_recv.at[2], down
    )

    @pl.when(rank < n - 1)
    def _():
        to_right.start()

    @pl.when(rank > 0)
    def _():
        to_left.start()
        move_left.start()

    @pl.when(rank == 0)
    def _():
        x[pl.ds(0, LEFT)] = jnp.zeros((LEFT, samples, width), BF16)

    @pl.when(rank == n - 1)
    def _():
        x[pl.ds(LEFT + own, RIGHT)] = jnp.zeros((RIGHT, samples, width), BF16)
        move_next[...] = jnp.zeros((8, 128), jnp.int32)

    rows = own + EXTRA
    reach = LEFT + own + LEFT
    margin = (KWIN - QBLOCK) // 2
    head_dim = width // ATOM_HEADS
    scale = 1.0 / math.sqrt(head_dim)

    def spread(first, count):
        part = x[pl.ds(first, count)].astype(F32).reshape(samples * count, width)
        atoms[pl.ds(samples * first, samples * count), :] = part

    def normed_rows(s, first, count):
        return normalize(atoms[pl.ds(samples * first + s, count, stride=samples), :]).astype(BF16)

    def window(first_row, row_count, first_key, key_count, moved):
        shape = (row_count, key_count)
        place = lax.broadcasted_iota(jnp.int32, shape, 1) + first_key
        query = lax.broadcasted_iota(jnp.int32, shape, 0) + first_row
        offset = place - ((query // QBLOCK) * QBLOCK + (LEFT - margin) + moved)
        absolute = place + (rank * own - LEFT)
        keep = (offset >= 0) & (offset < KWIN) & (absolute >= 0) & (absolute < n * own)
        return jnp.where(keep, 0.0, LOW)

    def attend(q, k, v, lowered):
        count, keys = lowered.shape
        lane_head = lax.broadcasted_iota(jnp.int32, (count, width), 1) // head_dim
        stacked = jnp.concatenate(
            [jnp.where(lane_head == h, q, 0.0) for h in range(ATOM_HEADS)], axis=0
        ).astype(BF16)
        score = dot_t(stacked, k).reshape(ATOM_HEADS, count, keys) * scale + lowered[None]
        expo = jnp.exp(score - jnp.max(score, axis=-1, keepdims=True))
        total = jnp.sum(expo, axis=-1, keepdims=True)
        mix = dot(expo.reshape(ATOM_HEADS * count, keys).astype(BF16), v)
        mix = mix.reshape(ATOM_HEADS, count, width) * (1.0 / total)
        merged = jnp.zeros((count, width), F32)
        for h in range(ATOM_HEADS):
            merged = jnp.where(lane_head == h, mix[h], merged)
        return merged.astype(BF16)

    load_x.wait()
    spread(LEFT, own)
    for copy in load_atom:
        copy.wait()
    q_own, k_own, v_own = [], [], []
    for s in range(samples):
        normed = normed_rows(s, LEFT, own)
        q_own.append(dot(normed, waq[...]))
        k_own.append(dot(normed, wak[...]).astype(BF16))
        v_own.append(dot(normed, wav[...]).astype(BF16))
    moved = [jnp.full((QBLOCK, reach), shift[b], jnp.int32) for b in range(own // QBLOCK)]
    window_own = window(0, own, 0, reach, jnp.concatenate(moved, axis=0))

    for copy in load_token:
        copy.wait()
    base = rank * tok_dev
    following = jnp.where(rank < n - 1, 0, -tokens)
    own_ids = ids[pl.ds(rank, 1), :]
    next_ids = ids[pl.ds(jnp.minimum(rank + 1, n - 1), 1), :][:, :EXTRA] + following
    row_ids = jnp.concatenate([own_ids, next_ids], axis=1) - base
    member = lax.broadcasted_iota(jnp.int32, (tok_dev, rows), 0) == row_ids
    member = jnp.where(member, 1.0, 0.0)
    share = 1.0 / jnp.sum(member, axis=1, keepdims=True)
    member = member.astype(BF16)
    given = tin[...].astype(F32).reshape(samples * tok_dev, tok_width)
    for c in range(tok_width // 128):
        inner[c] = given[:, c * 128 : (c + 1) * 128]
    here = pl.ds(pl.multiple_of(rank * tok_dev, tok_dev), tok_dev)

    @pl.when(rank > 0)
    def _():
        to_right.wait_recv()

    @pl.when(rank < n - 1)
    def _():
        to_left.wait_recv()
        move_left.wait_recv()

    spread(0, LEFT)
    spread(LEFT + own, RIGHT)
    behind = LEFT + own - LEFT
    ahead = LEFT + own + RIGHT - behind
    moved = jnp.broadcast_to(move_next[0:1, 0:1], (EXTRA, ahead))
    window_extra = window(own, EXTRA, behind, ahead, moved)

    def atom_mix(s):
        normed = jnp.concatenate(
            [normed_rows(s, 0, LEFT), normed_rows(s, LEFT + own, RIGHT)], axis=0
        )
        q = dot(normed[LEFT : LEFT + EXTRA], waq[...])
        k = dot(normed, wak[...]).astype(BF16)
        v = dot(normed, wav[...]).astype(BF16)
        k = jnp.concatenate([k[:LEFT], k_own[s], k[LEFT:]], axis=0)
        v = jnp.concatenate([v[:LEFT], v_own[s], v[LEFT:]], axis=0)
        return jnp.concatenate(
            [
                attend(q_own[s], k[:reach], v[:reach], window_own),
                attend(q, k[behind:], v[behind:], window_extra),
            ],
            axis=0,
        )

    sends = []

    def block_of(s, origin):
        return gathered.at[s, pl.ds(pl.multiple_of(origin * tok_dev, tok_dev), tok_dev), :]

    def send_block(s, origin, to):
        block = block_of(s, origin)
        copy = remote(
            block, block, gather_send.at[len(sends)], gather_recv.at[s * n + origin], to
        )
        copy.start()
        sends.append(copy)

    def await_block(s, origin):
        block = block_of(s, origin)
        remote(
            block, block, gather_send.at[0], gather_recv.at[s * n + origin], core_mate
        ).wait_recv()

    for s in range(samples):
        updated = atoms[pl.ds(LEFT * samples + s, rows, stride=samples), :]
        updated = (updated + dot(atom_mix(s), wao[...])).astype(BF16)
        atoms[pl.ds(LEFT * samples + s, rows, stride=samples), :] = updated.astype(F32)
        hidden = jnp.maximum(dot(updated, wtt[...]), 0.0)
        high = hidden.astype(BF16)
        low = (hidden - high.astype(F32)).astype(BF16)
        sums = dot(member, high) + dot(member, low)
        given = [
            inner[c, pl.ds(s, tok_dev, stride=samples), :] for c in range(tok_width // 128)
        ]
        fresh = (jnp.concatenate(given, axis=1) + sums * share).astype(BF16)
        state[s] = fresh
        gathered[s, here, :] = normalize(fresh.astype(F32)).astype(BF16)
        for d in range(1, outers):
            send_block(s, rank, device(flip(outer, d), mid, core))
        send_block(s, rank, mid_mate)
        send_block(s, rank, core_mate)

    tdim = tok_width // TOKEN_HEADS
    lane_token = lax.broadcasted_iota(jnp.int32, (tok_dev, tok_width), 1) // tdim

    def absorb(s):
        q = dot(gathered[s, here, :], wq[...])
        stacked = jnp.concatenate(
            [jnp.where(lane_token == h, q, 0.0) for h in range(TOKEN_HEADS)], axis=0
        ).astype(BF16)
        absorbed[s] = dot_t(stacked, wk[...]).astype(BF16)

    def bias_rows(first, count):
        wb_t = wb[...]
        lowered = jnp.where(mask[...] > 0, 0.0, LOW)
        for i in range(first, first + count):
            bias[:, i, :] = dot_t(wb_t, pair[i]) + lowered

    def relay_outer(s):
        for d in range(1, outers):
            origin = device(flip(outer, d), mid, core)
            await_block(s, origin)
            send_block(s, origin, mid_mate)
            send_block(s, origin, core_mate)

    def relay_mid(s):
        for d in range(outers):
            origin = device(flip(outer, d), 1 - mid, core)
            await_block(s, origin)
            send_block(s, origin, core_mate)

    load_wq.wait()
    load_wk.wait()
    for copy in load_pair:
        copy.wait()
    quarter = tok_dev // 4
    relay_outer(0)
    absorb(0)
    relay_outer(1)
    bias_rows(0, quarter)
    relay_mid(0)
    bias_rows(quarter, quarter)
    relay_mid(1)
    absorb(1)
    bias_rows(2 * quarter, 2 * quarter)
    atom_out[...] = (
        atoms[pl.ds(LEFT * samples, own * samples), :].reshape(own, samples, width).astype(BF16)
    )

    load_wv.wait()
    load_wo.wait()
    tscale = 1.0 / math.sqrt(tdim)
    for s in range(samples):
        for d in range(outers):
            for m in (mid, 1 - mid):
                await_block(s, device(flip(outer, d), m, 1 - core))
        score = dot_t(absorbed[s], gathered[s]) * tscale
        score = score + bias[...].reshape(TOKEN_HEADS * tok_dev, tokens)
        expo = jnp.exp(score - jnp.max(score, axis=-1, keepdims=True))
        total = jnp.sum(expo, axis=-1, keepdims=True)
        v = dot(gathered[s], wv[...]).astype(BF16)
        mix = dot(expo.astype(BF16), v) * (1.0 / total)
        merged = jnp.zeros((tok_dev, tok_width), F32)
        for h in range(TOKEN_HEADS):
            merged = jnp.where(lane_token == h, mix[h * tok_dev : (h + 1) * tok_dev], merged)
        result = state[s].astype(F32) + dot(merged.astype(BF16), wo[...])
        for c in range(tok_width // 128):
            inner[c, pl.ds(s, tok_dev, stride=samples), :] = result[:, c * 128 : (c + 1) * 128]
    result = jnp.concatenate([inner[c] for c in range(tok_width // 128)], axis=1)
    token_out[...] = result.reshape(tok_dev, samples, tok_width).astype(BF16)

    for copy in sends:
        copy.wait_send()

    @pl.when(rank < n - 1)
    def _():
        to_right.wait_send()

    @pl.when(rank > 0)
    def _():
        to_left.wait_send()
        move_left.wait_send()


def on_device(
    n,
    atom_feat,
    window_shift,
    atom_token,
    token_in,
    pair,
    key_mask,
    w_atom_query,
    w_atom_key,
    w_atom_value,
    w_atom_out,
    w_to_token,
    w_query,
    w_key,
    w_value,
    w_out,
    w_bias,
):
    own, samples, width = atom_feat.shape
    tok_dev, _, tok_width = token_in.shape
    tokens = pair.shape[1]
    ids = atom_token.reshape(n, own)
    mask = key_mask.reshape(1, tokens)
    big = (atom_feat, ids, token_in, pair, mask, w_atom_query, w_atom_key, w_atom_value, w_atom_out)
    big += (w_to_token, w_query, w_key, w_value, w_out, w_bias.T)
    buffers = [pltpu.VMEM(a.shape, a.dtype) for a in big]
    buffers[0] = pltpu.VMEM((LEFT + own + RIGHT, samples, width), BF16)
    atoms, toks = pl.pallas_call(
        functools.partial(kernel, n),
        out_shape=(
            pltpu.VMEM(atom_feat.shape, BF16),
            pltpu.VMEM(token_in.shape, BF16),
        ),
        in_specs=[pl.BlockSpec(memory_space=pltpu.SMEM)]
        + [pl.BlockSpec(memory_space=pltpu.HBM)] * len(big),
        out_specs=(
            pl.BlockSpec(memory_space=pltpu.VMEM),
            pl.BlockSpec(memory_space=pltpu.VMEM),
        ),
        scratch_shapes=buffers
        + [
            pltpu.VMEM((8 * (own // QBLOCK), 128), jnp.int32),
            pltpu.VMEM((8, 128), jnp.int32),
            pltpu.VMEM((TOKEN_HEADS, tok_dev, tokens), F32),
            pltpu.VMEM((samples * (LEFT + own + RIGHT), width), F32),
            pltpu.VMEM((tok_width // 128, samples * tok_dev, 128), F32),
            pltpu.VMEM((samples, tok_dev, tok_width), BF16),
            pltpu.VMEM((samples, TOKEN_HEADS * tok_dev, tok_width), BF16),
            pltpu.VMEM((samples, tokens, tok_width), BF16),
            pltpu.SemaphoreType.DMA((len(big),)),
            pltpu.SemaphoreType.DMA((3,)),
            pltpu.SemaphoreType.DMA((3,)),
            pltpu.SemaphoreType.DMA((samples * (n - 1),)),
            pltpu.SemaphoreType.DMA((samples * n,)),
        ],
        compiler_params=pltpu.CompilerParams(
            collective_id=0, has_side_effects=True, vmem_limit_bytes=48 * 1024 * 1024
        ),
    )(*[pltpu.with_memory_space_constraint(a, pltpu.HBM) for a in (window_shift, *big)])
    return atoms, toks


def solution(mesh):
    rows = P(("groups", "row"), None, None)
    return jax.shard_map(
        functools.partial(on_device, mesh.shape["row"]),
        mesh=mesh,
        in_specs=(rows, P(("groups", "row")), P("groups"), rows, rows, P("groups"))
        + (P(),) * 10,
        out_specs=(rows, rows),
        check_vma=False,
    )
```

```python
import functools
import math

import jax
import jax.numpy as jnp
from jax import lax
from jax.experimental import pallas as pl
from jax.experimental.pallas import tpu as pltpu
from jax.sharding import PartitionSpec as P

ATOM_HEADS = 4
QBLOCK = 32
KWIN = 128
SHIFT = 16
TOKEN_HEADS = 16
LEFT = 64
RIGHT = 96
EXTRA = 16
MESH = pl.DeviceIdType.MESH
F32 = jnp.float32
BF16 = jnp.bfloat16
LOW = -1e30


def dot(a, b):
    return jnp.dot(a, b, preferred_element_type=F32)


def dot_t(a, b):
    return lax.dot_general(a, b, (((1,), (1,)), ((), ())), preferred_element_type=F32)


def normalize(values):
    mean = jnp.mean(values, axis=-1, keepdims=True)
    centred = values - mean
    var = jnp.mean(centred * centred, axis=-1, keepdims=True)
    return centred * lax.rsqrt(var + 1e-05)


def flip(index, distance):
    result = index
    bit = 1
    while bit <= distance:
        if (distance // bit) % 2:
            result = result + bit - 2 * bit * ((index // bit) % 2)
        bit *= 2
    return result


def kernel(
    n,
    shift,
    x_in,
    ids_in,
    token_in,
    pair_in,
    mask_in,
    waq_in,
    wak_in,
    wav_in,
    wao_in,
    wtt_in,
    wq_in,
    wk_in,
    wv_in,
    wo_in,
    wb_in,
    atom_out,
    token_out,
    x,
    ids,
    tin,
    pair,
    mask,
    waq,
    wak,
    wav,
    wao,
    wtt,
    wq,
    wk,
    wv,
    wo,
    wb,
    move_own,
    move_next,
    bias,
    atoms,
    inner,
    state,
    absorbed,
    gathered,
    load_sem,
    halo_send,
    halo_recv,
    gather_send,
    gather_recv,
):
    rank = lax.axis_index("row")
    own = x_in.shape[0]
    width = waq_in.shape[0]
    samples = x_in.shape[1]
    tok_dev = token_in.shape[0]
    tok_width = wq_in.shape[0]
    tokens = n * tok_dev
    outers = n // 4
    core = rank % 2
    mid = (rank // 2) % 2
    outer = rank // 4

    def device(o, m, c):
        return (o * 2 + m) * 2 + c

    mid_mate = device(outer, 1 - mid, core)
    core_mate = device(outer, mid, 1 - core)

    loads = []

    def load(source, target):
        copy = pltpu.make_async_copy(source, target, load_sem.at[len(loads)])
        copy.start()
        loads.append(copy)
        return copy

    load_x = load(x_in, x.at[pl.ds(LEFT, own)])
    load_atom = [load(*p) for p in ((waq_in, waq), (wak_in, wak), (wav_in, wav))]
    load_token = [load(*p) for p in ((ids_in, ids), (token_in, tin), (wao_in, wao), (wtt_in, wtt))]

    barrier = pltpu.get_barrier_semaphore()
    partners = [(rank + 1) % n, (rank + n - 1) % n, mid_mate, core_mate]
    partners += [device(flip(outer, d), mid, core) for d in range(1, outers)]
    for partner in partners:
        pl.semaphore_signal(barrier, inc=1, device_id={"row": partner}, device_id_type=MESH)
    for b in range(own // QBLOCK):
        move_own[pl.ds(8 * b, 8), :] = jnp.full((8, 128), shift[b], jnp.int32)
    load_x.wait()
    pl.semaphore_wait(barrier, len(partners))

    def remote(source, target, send, recv, to):
        return pltpu.make_async_remote_copy(
            src_ref=source,
            dst_ref=target,
            send_sem=send,
            recv_sem=recv,
            device_id={"row": to},
            device_id_type=MESH,
        )

    up = (rank + 1) % n
    down = (rank + n - 1) % n
    to_right = remote(
        x.at[pl.ds(own, LEFT)], x.at[pl.ds(0, LEFT)], halo_send.at[0], halo_recv.at[0], up
    )
    to_left = remote(
        x.at[pl.ds(LEFT, RIGHT)],
        x.at[pl.ds(LEFT + own, RIGHT)],
        halo_send.at[1],
        halo_recv.at[1],
        down,
    )
    move_left = remote(
        move_own.at[pl.ds(0, 8)], move_next, halo_send.at[2], halo_recv.at[2], down
    )

    @pl.when(rank < n - 1)
    def _():
        to_right.start()

    @pl.when(rank > 0)
    def _():
        to_left.start()
        move_left.start()

    @pl.when(rank == 0)
    def _():
        x[pl.ds(0, LEFT)] = jnp.zeros((LEFT, samples, width), BF16)

    @pl.when(rank == n - 1)
    def _():
        x[pl.ds(LEFT + own, RIGHT)] = jnp.zeros((RIGHT, samples, width), BF16)
        move_next[...] = jnp.zeros((8, 128), jnp.int32)

    load_wq = load(wq_in, wq)
    load_wk = load(wk_in, wk)
    load_pair = [load(wb_in, wb), load(mask_in, mask), load(pair_in, pair)]
    load_wv = load(wv_in, wv)
    load_wo = load(wo_in, wo)

    rows = own + EXTRA
    reach = LEFT + own + LEFT
    margin = (KWIN - QBLOCK) // 2
    head_dim = width // ATOM_HEADS
    scale = 1.0 / math.sqrt(head_dim)

    def spread(first, count):
        part = x[pl.ds(first, count)].astype(F32).reshape(samples * count, width)
        atoms[pl.ds(samples * first, samples * count), :] = part

    def normed_rows(s, first, count):
        return normalize(atoms[pl.ds(samples * first + s, count, stride=samples), :]).astype(BF16)

    def window(first_row, row_count, first_key, key_count, moved):
        shape = (row_count, key_count)
        place = lax.broadcasted_iota(jnp.int32, shape, 1) + first_key
        query = lax.broadcasted_iota(jnp.int32, shape, 0) + first_row
        offset = place - ((query // QBLOCK) * QBLOCK + (LEFT - margin) + moved)
        absolute = place + (rank * own - LEFT)
        keep = (offset >= 0) & (offset < KWIN) & (absolute >= 0) & (absolute < n * own)
        return jnp.where(keep, 0.0, LOW)

    def attend(q, k, v, lowered):
        count, keys = lowered.shape
        lane_head = lax.broadcasted_iota(jnp.int32, (count, width), 1) // head_dim
        stacked = jnp.concatenate(
            [jnp.where(lane_head == h, q, 0.0) for h in range(ATOM_HEADS)], axis=0
        ).astype(BF16)
        score = dot_t(stacked, k).reshape(ATOM_HEADS, count, keys) * scale + lowered[None]
        expo = jnp.exp(score - jnp.max(score, axis=-1, keepdims=True))
        total = jnp.sum(expo, axis=-1, keepdims=True)
        mix = dot(expo.reshape(ATOM_HEADS * count, keys).astype(BF16), v)
        mix = mix.reshape(ATOM_HEADS, count, width) * (1.0 / total)
        merged = jnp.zeros((count, width), F32)
        for h in range(ATOM_HEADS):
            merged = jnp.where(lane_head == h, mix[h], merged)
        return merged.astype(BF16)

    spread(LEFT, own)
    for copy in load_atom:
        copy.wait()
    q_own, k_own, v_own = [], [], []
    for s in range(samples):
        normed = normed_rows(s, LEFT, own)
        q_own.append(dot(normed, waq[...]))
        k_own.append(dot(normed, wak[...]).astype(BF16))
        v_own.append(dot(normed, wav[...]).astype(BF16))
    moved = [jnp.full((QBLOCK, reach), shift[b], jnp.int32) for b in range(own // QBLOCK)]
    window_own = window(0, own, 0, reach, jnp.concatenate(moved, axis=0))

    for copy in load_token:
        copy.wait()
    base = rank * tok_dev
    following = jnp.where(rank < n - 1, 0, -tokens)
    own_ids = ids[pl.ds(rank, 1), :]
    next_ids = ids[pl.ds(jnp.minimum(rank + 1, n - 1), 1), :][:, :EXTRA] + following
    row_ids = jnp.concatenate([own_ids, next_ids], axis=1) - base
    member = lax.broadcasted_iota(jnp.int32, (tok_dev, rows), 0) == row_ids
    member = jnp.where(member, 1.0, 0.0)
    share = 1.0 / jnp.sum(member, axis=1, keepdims=True)
    member = member.astype(BF16)
    given = tin[...].astype(F32).reshape(samples * tok_dev, tok_width)
    for c in range(tok_width // 128):
        inner[c] = given[:, c * 128 : (c + 1) * 128]
    here = pl.ds(pl.multiple_of(rank * tok_dev, tok_dev), tok_dev)

    @pl.when(rank > 0)
    def _():
        to_right.wait_recv()

    @pl.when(rank < n - 1)
    def _():
        to_left.wait_recv()
        move_left.wait_recv()

    spread(0, LEFT)
    spread(LEFT + own, RIGHT)
    behind = LEFT + own - LEFT
    ahead = LEFT + own + RIGHT - behind
    moved = jnp.broadcast_to(move_next[0:1, 0:1], (EXTRA, ahead))
    window_extra = window(own, EXTRA, behind, ahead, moved)

    def atom_mix(s):
        normed = jnp.concatenate(
            [normed_rows(s, 0, LEFT), normed_rows(s, LEFT + own, RIGHT)], axis=0
        )
        q = dot(normed[LEFT : LEFT + EXTRA], waq[...])
        k = dot(normed, wak[...]).astype(BF16)
        v = dot(normed, wav[...]).astype(BF16)
        k = jnp.concatenate([k[:LEFT], k_own[s], k[LEFT:]], axis=0)
        v = jnp.concatenate([v[:LEFT], v_own[s], v[LEFT:]], axis=0)
        return jnp.concatenate(
            [
                attend(q_own[s], k[:reach], v[:reach], window_own),
                attend(q, k[behind:], v[behind:], window_extra),
            ],
            axis=0,
        )

    sends = []

    def block_of(s, origin):
        return gathered.at[s, pl.ds(pl.multiple_of(origin * tok_dev, tok_dev), tok_dev), :]

    def send_block(s, origin, to):
        block = block_of(s, origin)
        copy = remote(
            block, block, gather_send.at[len(sends)], gather_recv.at[s * n + origin], to
        )
        copy.start()
        sends.append(copy)

    def await_block(s, origin):
        block = block_of(s, origin)
        remote(
            block, block, gather_send.at[0], gather_recv.at[s * n + origin], core_mate
        ).wait_recv()

    for s in range(samples):
        updated = atoms[pl.ds(LEFT * samples + s, rows, stride=samples), :]
        updated = (updated + dot(atom_mix(s), wao[...])).astype(BF16)
        atoms[pl.ds(LEFT * samples + s, rows, stride=samples), :] = updated.astype(F32)
        hidden = jnp.maximum(dot(updated, wtt[...]), 0.0)
        high = hidden.astype(BF16)
        low = (hidden - high.astype(F32)).astype(BF16)
        sums = dot(member, high) + dot(member, low)
        given = [
            inner[c, pl.ds(s, tok_dev, stride=samples), :] for c in range(tok_width // 128)
        ]
        fresh = (jnp.concatenate(given, axis=1) + sums * share).astype(BF16)
        state[s] = fresh
        gathered[s, here, :] = normalize(fresh.astype(F32)).astype(BF16)
        for d in range(1, outers):
            send_block(s, rank, device(flip(outer, d), mid, core))
        send_block(s, rank, mid_mate)
        send_block(s, rank, core_mate)

    tdim = tok_width // TOKEN_HEADS
    lane_token = lax.broadcasted_iota(jnp.int32, (tok_dev, tok_width), 1) // tdim

    def absorb(s):
        q = dot(gathered[s, here, :], wq[...])
        stacked = jnp.concatenate(
            [jnp.where(lane_token == h, q, 0.0) for h in range(TOKEN_HEADS)], axis=0
        ).astype(BF16)
        absorbed[s] = dot_t(stacked, wk[...]).astype(BF16)

    def bias_rows(first, count):
        wb_t = wb[...]
        lowered = jnp.where(mask[...] > 0, 0.0, LOW)

        @pl.loop(first, first + count)
        def _(i):
            row = dot_t(wb_t, pair[i]) + lowered
            bias[:, pl.ds(i, 1), :] = row.reshape(TOKEN_HEADS, 1, tokens)

    def relay_outer(s):
        for d in range(1, outers):
            origin = device(flip(outer, d), mid, core)
            await_block(s, origin)
            send_block(s, origin, mid_mate)
            send_block(s, origin, core_mate)

    def relay_mid(s):
        for d in range(outers):
            origin = device(flip(outer, d), 1 - mid, core)
            await_block(s, origin)
            send_block(s, origin, core_mate)

    load_wq.wait()
    load_wk.wait()
    for copy in load_pair:
        copy.wait()
    quarter = tok_dev // 4
    relay_outer(0)
    absorb(0)
    relay_outer(1)
    bias_rows(0, quarter)
    relay_mid(0)
    bias_rows(quarter, quarter)
    relay_mid(1)
    absorb(1)
    bias_rows(2 * quarter, 2 * quarter)
    atom_out[...] = (
        atoms[pl.ds(LEFT * samples, own * samples), :].reshape(own, samples, width).astype(BF16)
    )

    load_wv.wait()
    load_wo.wait()
    tscale = 1.0 / math.sqrt(tdim)
    @pl.loop(0, samples)
    def _(s):
        for d in range(outers):
            for m in (mid, 1 - mid):
                await_block(s, device(flip(outer, d), m, 1 - core))
        score = dot_t(absorbed[s], gathered[s]) * tscale
        score = score + bias[...].reshape(TOKEN_HEADS * tok_dev, tokens)
        expo = jnp.exp(score - jnp.max(score, axis=-1, keepdims=True))
        total = jnp.sum(expo, axis=-1, keepdims=True)
        v = dot(gathered[s], wv[...]).astype(BF16)
        mix = dot(expo.astype(BF16), v) * (1.0 / total)
        merged = jnp.zeros((tok_dev, tok_width), F32)
        for h in range(TOKEN_HEADS):
            merged = jnp.where(lane_token == h, mix[h * tok_dev : (h + 1) * tok_dev], merged)
        result = state[s].astype(F32) + dot(merged.astype(BF16), wo[...])
        for c in range(tok_width // 128):
            inner[c, pl.ds(s, tok_dev, stride=samples), :] = result[:, c * 128 : (c + 1) * 128]

    result = jnp.concatenate([inner[c] for c in range(tok_width // 128)], axis=1)
    token_out[...] = result.reshape(tok_dev, samples, tok_width).astype(BF16)

    for copy in sends:
        copy.wait_send()

    @pl.when(rank < n - 1)
    def _():
        to_right.wait_send()

    @pl.when(rank > 0)
    def _():
        to_left.wait_send()
        move_left.wait_send()


def on_device(
    n,
    atom_feat,
    window_shift,
    atom_token,
    token_in,
    pair,
    key_mask,
    w_atom_query,
    w_atom_key,
    w_atom_value,
    w_atom_out,
    w_to_token,
    w_query,
    w_key,
    w_value,
    w_out,
    w_bias,
):
    own, samples, width = atom_feat.shape
    tok_dev, _, tok_width = token_in.shape
    tokens = pair.shape[1]
    ids = atom_token.reshape(n, own)
    mask = key_mask.reshape(1, tokens)
    big = (atom_feat, ids, token_in, pair, mask, w_atom_query, w_atom_key, w_atom_value, w_atom_out)
    big += (w_to_token, w_query, w_key, w_value, w_out, w_bias.T)
    buffers = [pltpu.VMEM(a.shape, a.dtype) for a in big]
    buffers[0] = pltpu.VMEM((LEFT + own + RIGHT, samples, width), BF16)
    atoms, toks = pl.pallas_call(
        functools.partial(kernel, n),
        out_shape=(
            pltpu.VMEM(atom_feat.shape, BF16),
            pltpu.VMEM(token_in.shape, BF16),
        ),
        in_specs=[pl.BlockSpec(memory_space=pltpu.SMEM)]
        + [pl.BlockSpec(memory_space=pltpu.HBM)] * len(big),
        out_specs=(
            pl.BlockSpec(memory_space=pltpu.VMEM),
            pl.BlockSpec(memory_space=pltpu.VMEM),
        ),
        scratch_shapes=buffers
        + [
            pltpu.VMEM((8 * (own // QBLOCK), 128), jnp.int32),
            pltpu.VMEM((8, 128), jnp.int32),
            pltpu.VMEM((TOKEN_HEADS, tok_dev, tokens), F32),
            pltpu.VMEM((samples * (LEFT + own + RIGHT), width), F32),
            pltpu.VMEM((tok_width // 128, samples * tok_dev, 128), F32),
            pltpu.VMEM((samples, tok_dev, tok_width), BF16),
            pltpu.VMEM((samples, TOKEN_HEADS * tok_dev, tok_width), BF16),
            pltpu.VMEM((samples, tokens, tok_width), BF16),
            pltpu.SemaphoreType.DMA((len(big),)),
            pltpu.SemaphoreType.DMA((3,)),
            pltpu.SemaphoreType.DMA((3,)),
            pltpu.SemaphoreType.DMA((samples * (n - 1),)),
            pltpu.SemaphoreType.DMA((samples * n,)),
        ],
        compiler_params=pltpu.CompilerParams(
            collective_id=0, has_side_effects=True, vmem_limit_bytes=48 * 1024 * 1024
        ),
    )(*[pltpu.with_memory_space_constraint(a, pltpu.HBM) for a in (window_shift, *big)])
    return atoms, toks


def solution(mesh):
    rows = P(("groups", "row"), None, None)
    return jax.shard_map(
        functools.partial(on_device, mesh.shape["row"]),
        mesh=mesh,
        in_specs=(rows, P(("groups", "row")), P("groups"), rows, rows, P("groups"))
        + (P(),) * 10,
        out_specs=(rows, rows),
        check_vma=False,
    )
```

```python
import functools
import math

import jax
import jax.numpy as jnp
from jax import lax
from jax.experimental import pallas as pl
from jax.experimental.pallas import tpu as pltpu
from jax.sharding import PartitionSpec as P

ATOM_HEADS = 4
QBLOCK = 32
KWIN = 128
SHIFT = 16
TOKEN_HEADS = 16
LEFT = 64
RIGHT = 96
EXTRA = 16
MESH = pl.DeviceIdType.MESH
F32 = jnp.float32
BF16 = jnp.bfloat16
LOW = -1e30


def dot(a, b):
    return jnp.dot(a, b, preferred_element_type=F32)


def dot_t(a, b):
    return lax.dot_general(a, b, (((1,), (1,)), ((), ())), preferred_element_type=F32)


def normalize(values):
    mean = jnp.mean(values, axis=-1, keepdims=True)
    centred = values - mean
    var = jnp.mean(centred * centred, axis=-1, keepdims=True)
    return centred * lax.rsqrt(var + 1e-05)


def flip(index, distance):
    result = index
    bit = 1
    while bit <= distance:
        if (distance // bit) % 2:
            result = result + bit - 2 * bit * ((index // bit) % 2)
        bit *= 2
    return result


def kernel(
    n,
    shift,
    x_in,
    ids_in,
    token_in,
    pair_in,
    mask_in,
    waq_in,
    wak_in,
    wav_in,
    wao_in,
    wtt_in,
    wq_in,
    wk_in,
    wv_in,
    wo_in,
    wb_in,
    atom_out,
    token_out,
    x,
    ids,
    tin,
    pair,
    mask,
    waq,
    wak,
    wav,
    wao,
    wtt,
    wq,
    wk,
    wv,
    wo,
    wb,
    move_own,
    move_next,
    bias,
    atoms,
    inner,
    state,
    absorbed,
    gathered,
    load_sem,
    halo_send,
    halo_recv,
    gather_send,
    gather_recv,
):
    rank = lax.axis_index("row")
    own = x_in.shape[0]
    width = waq_in.shape[0]
    samples = x_in.shape[1]
    tok_dev = token_in.shape[0]
    tok_width = wq_in.shape[0]
    tokens = n * tok_dev
    outers = n // 4
    core = rank % 2
    mid = (rank // 2) % 2
    outer = rank // 4

    def device(o, m, c):
        return (o * 2 + m) * 2 + c

    mid_mate = device(outer, 1 - mid, core)
    core_mate = device(outer, mid, 1 - core)

    loads = []

    def load(source, target):
        copy = pltpu.make_async_copy(source, target, load_sem.at[len(loads)])
        copy.start()
        loads.append(copy)
        return copy

    load_x = load(x_in, x.at[pl.ds(LEFT, own)])
    load_atom = [load(*p) for p in ((waq_in, waq), (wak_in, wak), (wav_in, wav))]
    load_token = [load(*p) for p in ((ids_in, ids), (token_in, tin), (wao_in, wao), (wtt_in, wtt))]

    barrier = pltpu.get_barrier_semaphore()
    partners = [(rank + 1) % n, (rank + n - 1) % n, mid_mate, core_mate]
    partners += [device(flip(outer, d), mid, core) for d in range(1, outers)]
    for partner in partners:
        pl.semaphore_signal(barrier, inc=1, device_id={"row": partner}, device_id_type=MESH)
    for b in range(own // QBLOCK):
        move_own[pl.ds(8 * b, 8), :] = jnp.full((8, 128), shift[b], jnp.int32)
    load_x.wait()
    pl.semaphore_wait(barrier, len(partners))

    def remote(source, target, send, recv, to):
        return pltpu.make_async_remote_copy(
            src_ref=source,
            dst_ref=target,
            send_sem=send,
            recv_sem=recv,
            device_id={"row": to},
            device_id_type=MESH,
        )

    up = (rank + 1) % n
    down = (rank + n - 1) % n
    to_right = remote(
        x.at[pl.ds(own, LEFT)], x.at[pl.ds(0, LEFT)], halo_send.at[0], halo_recv.at[0], up
    )
    to_left = remote(
        x.at[pl.ds(LEFT, RIGHT)],
        x.at[pl.ds(LEFT + own, RIGHT)],
        halo_send.at[1],
        halo_recv.at[1],
        down,
    )
    move_left = remote(
        move_own.at[pl.ds(0, 8)], move_next, halo_send.at[2], halo_recv.at[2], down
    )

    @pl.when(rank < n - 1)
    def _():
        to_right.start()

    @pl.when(rank > 0)
    def _():
        to_left.start()
        move_left.start()

    @pl.when(rank == 0)
    def _():
        x[pl.ds(0, LEFT)] = jnp.zeros((LEFT, samples, width), BF16)

    @pl.when(rank == n - 1)
    def _():
        x[pl.ds(LEFT + own, RIGHT)] = jnp.zeros((RIGHT, samples, width), BF16)
        move_next[...] = jnp.zeros((8, 128), jnp.int32)

    load_pair = [load(wb_in, wb), load(mask_in, mask), load(pair_in, pair)]
    load_wq = load(wq_in, wq)
    load_wk = load(wk_in, wk)
    load_wv = load(wv_in, wv)
    load_wo = load(wo_in, wo)

    rows = own + EXTRA
    reach = LEFT + own + LEFT
    margin = (KWIN - QBLOCK) // 2
    head_dim = width // ATOM_HEADS
    scale = 1.0 / math.sqrt(head_dim)

    def spread(first, count):
        part = x[pl.ds(first, count)].astype(F32).reshape(samples * count, width)
        atoms[pl.ds(samples * first, samples * count), :] = part

    def normed_rows(s, first, count):
        return normalize(atoms[pl.ds(samples * first + s, count, stride=samples), :]).astype(BF16)

    def window(first_row, row_count, first_key, key_count, moved):
        shape = (row_count, key_count)
        place = lax.broadcasted_iota(jnp.int32, shape, 1) + first_key
        query = lax.broadcasted_iota(jnp.int32, shape, 0) + first_row
        offset = place - ((query // QBLOCK) * QBLOCK + (LEFT - margin) + moved)
        absolute = place + (rank * own - LEFT)
        keep = (offset >= 0) & (offset < KWIN) & (absolute >= 0) & (absolute < n * own)
        return jnp.where(keep, 0.0, LOW)

    def attend(q, k, v, lowered):
        count, keys = lowered.shape
        lane_head = lax.broadcasted_iota(jnp.int32, (count, width), 1) // head_dim
        stacked = jnp.concatenate(
            [jnp.where(lane_head == h, q, 0.0) for h in range(ATOM_HEADS)], axis=0
        ).astype(BF16)
        score = dot_t(stacked, k).reshape(ATOM_HEADS, count, keys) * scale + lowered[None]
        expo = jnp.exp(score - jnp.max(score, axis=-1, keepdims=True))
        total = jnp.sum(expo, axis=-1, keepdims=True)
        mix = dot(expo.reshape(ATOM_HEADS * count, keys).astype(BF16), v)
        mix = mix.reshape(ATOM_HEADS, count, width) * (1.0 / total)
        merged = jnp.zeros((count, width), F32)
        for h in range(ATOM_HEADS):
            merged = jnp.where(lane_head == h, mix[h], merged)
        return merged.astype(BF16)

    spread(LEFT, own)
    for copy in load_atom:
        copy.wait()
    q_own, k_own, v_own = [], [], []
    for s in range(samples):
        normed = normed_rows(s, LEFT, own)
        q_own.append(dot(normed, waq[...]))
        k_own.append(dot(normed, wak[...]).astype(BF16))
        v_own.append(dot(normed, wav[...]).astype(BF16))
    moved = [jnp.full((QBLOCK, reach), shift[b], jnp.int32) for b in range(own // QBLOCK)]
    window_own = window(0, own, 0, reach, jnp.concatenate(moved, axis=0))

    for copy in load_token:
        copy.wait()
    base = rank * tok_dev
    following = jnp.where(rank < n - 1, 0, -tokens)
    own_ids = ids[pl.ds(rank, 1), :]
    next_ids = ids[pl.ds(jnp.minimum(rank + 1, n - 1), 1), :][:, :EXTRA] + following
    row_ids = jnp.concatenate([own_ids, next_ids], axis=1) - base
    member = lax.broadcasted_iota(jnp.int32, (tok_dev, rows), 0) == row_ids
    member = jnp.where(member, 1.0, 0.0)
    share = 1.0 / jnp.sum(member, axis=1, keepdims=True)
    member = member.astype(BF16)
    given = tin[...].astype(F32).reshape(samples * tok_dev, tok_width)
    for c in range(tok_width // 128):
        inner[c] = given[:, c * 128 : (c + 1) * 128]
    here = pl.ds(pl.multiple_of(rank * tok_dev, tok_dev), tok_dev)

    def bias_rows(first, count):
        wb_t = wb[...]
        lowered = jnp.where(mask[...] > 0, 0.0, LOW)
        for i in range(first, first + count):
            bias[:, i, :] = dot_t(wb_t, pair[i]) + lowered

    for copy in load_pair:
        copy.wait()
    quarter = tok_dev // 4
    bias_rows(0, 2 * quarter)

    @pl.when(rank > 0)
    def _():
        to_right.wait_recv()

    @pl.when(rank < n - 1)
    def _():
        to_left.wait_recv()
        move_left.wait_recv()

    spread(0, LEFT)
    spread(LEFT + own, RIGHT)
    behind = LEFT + own - LEFT
    ahead = LEFT + own + RIGHT - behind
    moved = jnp.broadcast_to(move_next[0:1, 0:1], (EXTRA, ahead))
    window_extra = window(own, EXTRA, behind, ahead, moved)

    def atom_mix(s):
        normed = jnp.concatenate(
            [normed_rows(s, 0, LEFT), normed_rows(s, LEFT + own, RIGHT)], axis=0
        )
        q = dot(normed[LEFT : LEFT + EXTRA], waq[...])
        k = dot(normed, wak[...]).astype(BF16)
        v = dot(normed, wav[...]).astype(BF16)
        k = jnp.concatenate([k[:LEFT], k_own[s], k[LEFT:]], axis=0)
        v = jnp.concatenate([v[:LEFT], v_own[s], v[LEFT:]], axis=0)
        return jnp.concatenate(
            [
                attend(q_own[s], k[:reach], v[:reach], window_own),
                attend(q, k[behind:], v[behind:], window_extra),
            ],
            axis=0,
        )

    sends = []

    def block_of(s, origin):
        return gathered.at[s, pl.ds(pl.multiple_of(origin * tok_dev, tok_dev), tok_dev), :]

    def send_block(s, origin, to):
        block = block_of(s, origin)
        copy = remote(
            block, block, gather_send.at[len(sends)], gather_recv.at[s * n + origin], to
        )
        copy.start()
        sends.append(copy)

    def await_block(s, origin):
        block = block_of(s, origin)
        remote(
            block, block, gather_send.at[0], gather_recv.at[s * n + origin], core_mate
        ).wait_recv()

    for s in range(samples):
        updated = atoms[pl.ds(LEFT * samples + s, rows, stride=samples), :]
        updated = (updated + dot(atom_mix(s), wao[...])).astype(BF16)
        atoms[pl.ds(LEFT * samples + s, rows, stride=samples), :] = updated.astype(F32)
        hidden = jnp.maximum(dot(updated, wtt[...]), 0.0)
        high = hidden.astype(BF16)
        low = (hidden - high.astype(F32)).astype(BF16)
        sums = dot(member, high) + dot(member, low)
        given = [
            inner[c, pl.ds(s, tok_dev, stride=samples), :] for c in range(tok_width // 128)
        ]
        fresh = (jnp.concatenate(given, axis=1) + sums * share).astype(BF16)
        state[s] = fresh
        gathered[s, here, :] = normalize(fresh.astype(F32)).astype(BF16)
        for d in range(1, outers):
            send_block(s, rank, device(flip(outer, d), mid, core))
        send_block(s, rank, mid_mate)
        send_block(s, rank, core_mate)

    tdim = tok_width // TOKEN_HEADS
    lane_token = lax.broadcasted_iota(jnp.int32, (tok_dev, tok_width), 1) // tdim

    def absorb(s):
        q = dot(gathered[s, here, :], wq[...])
        stacked = jnp.concatenate(
            [jnp.where(lane_token == h, q, 0.0) for h in range(TOKEN_HEADS)], axis=0
        ).astype(BF16)
        absorbed[s] = dot_t(stacked, wk[...]).astype(BF16)

    def relay_outer(s):
        for d in range(1, outers):
            origin = device(flip(outer, d), mid, core)
            await_block(s, origin)
            send_block(s, origin, mid_mate)
            send_block(s, origin, core_mate)

    def relay_mid(s):
        for d in range(outers):
            origin = device(flip(outer, d), 1 - mid, core)
            await_block(s, origin)
            send_block(s, origin, core_mate)

    relay_outer(0)
    load_wq.wait()
    load_wk.wait()
    absorb(0)
    relay_outer(1)
    bias_rows(2 * quarter, quarter)
    relay_mid(0)
    bias_rows(3 * quarter, quarter)
    relay_mid(1)
    absorb(1)
    atom_out[...] = (
        atoms[pl.ds(LEFT * samples, own * samples), :].reshape(own, samples, width).astype(BF16)
    )

    load_wv.wait()
    load_wo.wait()
    tscale = 1.0 / math.sqrt(tdim)
    for s in range(samples):
        for d in range(outers):
            for m in (mid, 1 - mid):
                await_block(s, device(flip(outer, d), m, 1 - core))
        score = dot_t(absorbed[s], gathered[s]) * tscale
        score = score + bias[...].reshape(TOKEN_HEADS * tok_dev, tokens)
        expo = jnp.exp(score - jnp.max(score, axis=-1, keepdims=True))
        total = jnp.sum(expo, axis=-1, keepdims=True)
        v = dot(gathered[s], wv[...]).astype(BF16)
        mix = dot(expo.astype(BF16), v) * (1.0 / total)
        merged = jnp.zeros((tok_dev, tok_width), F32)
        for h in range(TOKEN_HEADS):
            merged = jnp.where(lane_token == h, mix[h * tok_dev : (h + 1) * tok_dev], merged)
        result = state[s].astype(F32) + dot(merged.astype(BF16), wo[...])
        for c in range(tok_width // 128):
            inner[c, pl.ds(s, tok_dev, stride=samples), :] = result[:, c * 128 : (c + 1) * 128]

    result = jnp.concatenate([inner[c] for c in range(tok_width // 128)], axis=1)
    token_out[...] = result.reshape(tok_dev, samples, tok_width).astype(BF16)

    for copy in sends:
        copy.wait_send()

    @pl.when(rank < n - 1)
    def _():
        to_right.wait_send()

    @pl.when(rank > 0)
    def _():
        to_left.wait_send()
        move_left.wait_send()


def on_device(
    n,
    atom_feat,
    window_shift,
    atom_token,
    token_in,
    pair,
    key_mask,
    w_atom_query,
    w_atom_key,
    w_atom_value,
    w_atom_out,
    w_to_token,
    w_query,
    w_key,
    w_value,
    w_out,
    w_bias,
):
    own, samples, width = atom_feat.shape
    tok_dev, _, tok_width = token_in.shape
    tokens = pair.shape[1]
    ids = atom_token.reshape(n, own)
    mask = key_mask.reshape(1, tokens)
    big = (atom_feat, ids, token_in, pair, mask, w_atom_query, w_atom_key, w_atom_value, w_atom_out)
    big += (w_to_token, w_query, w_key, w_value, w_out, w_bias.T)
    buffers = [pltpu.VMEM(a.shape, a.dtype) for a in big]
    buffers[0] = pltpu.VMEM((LEFT + own + RIGHT, samples, width), BF16)
    atoms, toks = pl.pallas_call(
        functools.partial(kernel, n),
        out_shape=(
            pltpu.VMEM(atom_feat.shape, BF16),
            pltpu.VMEM(token_in.shape, BF16),
        ),
        in_specs=[pl.BlockSpec(memory_space=pltpu.SMEM)]
        + [pl.BlockSpec(memory_space=pltpu.HBM)] * len(big),
        out_specs=(
            pl.BlockSpec(memory_space=pltpu.VMEM),
            pl.BlockSpec(memory_space=pltpu.VMEM),
        ),
        scratch_shapes=buffers
        + [
            pltpu.VMEM((8 * (own // QBLOCK), 128), jnp.int32),
            pltpu.VMEM((8, 128), jnp.int32),
            pltpu.VMEM((TOKEN_HEADS, tok_dev, tokens), F32),
            pltpu.VMEM((samples * (LEFT + own + RIGHT), width), F32),
            pltpu.VMEM((tok_width // 128, samples * tok_dev, 128), F32),
            pltpu.VMEM((samples, tok_dev, tok_width), BF16),
            pltpu.VMEM((samples, TOKEN_HEADS * tok_dev, tok_width), BF16),
            pltpu.VMEM((samples, tokens, tok_width), BF16),
            pltpu.SemaphoreType.DMA((len(big),)),
            pltpu.SemaphoreType.DMA((3,)),
            pltpu.SemaphoreType.DMA((3,)),
            pltpu.SemaphoreType.DMA((samples * (n - 1),)),
            pltpu.SemaphoreType.DMA((samples * n,)),
        ],
        compiler_params=pltpu.CompilerParams(
            collective_id=0, has_side_effects=True, vmem_limit_bytes=48 * 1024 * 1024
        ),
    )(*[pltpu.with_memory_space_constraint(a, pltpu.HBM) for a in (window_shift, *big)])
    return atoms, toks


def solution(mesh):
    rows = P(("groups", "row"), None, None)
    return jax.shard_map(
        functools.partial(on_device, mesh.shape["row"]),
        mesh=mesh,
        in_specs=(rows, P(("groups", "row")), P("groups"), rows, rows, P("groups"))
        + (P(),) * 10,
        out_specs=(rows, rows),
        check_vma=False,
    )
```
